512 devices in a mesh: row: 8 (over z), col: 16 (over y, core), layer: 4 (over x).
Axes of the slice: x: 4, y: 8, z: 8, core: 2. Of those that a mesh axis runs over, the one named last changes fastest.
Arguments:
- matrix: bfloat16 [8192, 8192], P('row', ('col', 'layer')), may hold values from -6 to 6
- list_x: int32 [256, 40], P('row'), may hold values from 0 to 255, all different within a row; in each aligned block of 32 rows (0 to 31, 32 to 63, ...) at most 10 rows name the same one
- list_sq: int32 [256, 60], P('row'), may hold values from 0 to 255, all different within a row
- list_out: int32 [256, 40], P('row'), may hold values from 0 to 255, all different within a row
Outputs:
- updated: bfloat16 [8192, 8192], P('row', ('col', 'layer'))
The draws below stay inside these ranges and needn't reach their ends.
Inputs may be any that keep to these rules, and one draw needn't show every extreme that they name: `list_x`: each row holds distinct block column numbers; within each aligned group of 32 block rows (the rows of one device along row) no block column appears in more than 10 rows. `list_sq`: each row holds distinct block column numbers. `list_out`: each row holds distinct block column numbers.
All inputs are finite; a program needn't handle non-finite values.
Results may differ from the reference program's by a relative error of at most 0.004.
Values may be sent and summed in bfloat16 or wider, within the bound.
No kernel may reach another device: no remote copies, remote signals or barrier semaphores. Data moves between devices by JAX's collectives and lax.ppermute only.
A program may use at most 128 MiB of HBM per device.

```python
import math
import jax
import jax.numpy as jnp
import numpy as np
from jax import lax

B = 32
NB = 256
KX = 40
KSQ = 60
M = 8192
RB = 32
CAPX = 10


def block_scale(key, dims, shards, low, largest):
    factor_of, own = 1.0, jax.random.fold_in(key, 6)
    for dim, shards_of in shards:
        steps = jnp.exp(jax.random.uniform(jax.random.fold_in(own, dim), (shards_of,), jnp.float32, low / len(shards), largest / len(shards)))
        factor_of = factor_of * jnp.repeat(steps, dims[dim] // shards_of).reshape([-1 if axis == dim else 1 for axis in range(len(dims))])
    return factor_of


def different_ones(key, rows, number_of, top, lift):
    order = jax.random.permutation(jax.random.fold_in(key, 1), number_of)
    favour = order
    for power in range(3):
        favour = favour * favour // number_of
    favour = favour * lift // number_of
    chance = jax.random.randint(jax.random.fold_in(key, 2), (rows, number_of), 0, 4096) + favour
    holders = jax.random.permutation(jax.random.fold_in(key, 3), rows)[jnp.arange(number_of) % rows]
    chance = jnp.where(jnp.arange(rows)[:, None] == holders[None, :], 1 << 14, chance)
    merit = chance * number_of + jnp.arange(number_of)
    return lax.top_k(merit.astype(jnp.int32), top)[1].astype(jnp.int32)


def routed_block(rng, own, number, rows, count, top, bound, slope):
    ranking = jax.random.permutation(rng, count)
    packed, ordinary = portions_of(count, rows * top, bound, slope, True), portions_of(count, rows * top, bound, slope, False)
    places = jnp.arange(count)

    def named(tallies, turn):
        used = int((tallies > 0).sum())
        fixed = max(1, used // 4)
        moved = fixed + (places - fixed + turn * (used - fixed)) % max(1, count - fixed)
        return jnp.zeros((count,), jnp.int32).at[ranking[jnp.where(places < fixed, places, moved)]].set(jnp.asarray(tallies, jnp.int32))

    tallies = jnp.where(number % 4 == 0, named(packed, number // 4), named(ordinary, number - number // 4 - 1))
    mixed = jax.random.permutation(jax.random.fold_in(own, 3), count)
    giver, taker = mixed[0:count // 2 * 2:2], mixed[1:count // 2 * 2:2]
    room = jnp.minimum(tallies[giver] - 1, bound - tallies[taker]) // 2
    room = jnp.where((giver == ranking[0]) | (taker == ranking[0]) | (tallies[taker] == 0), 0, jnp.maximum(room, 0))
    moved = jax.random.randint(jax.random.fold_in(own, 4), (count // 2,), 0, 1 << 20) % (room + 1)
    tallies = tallies.at[giver].add(-moved).at[taker].add(moved)
    labels = jnp.searchsorted(jnp.cumsum(tallies), jnp.arange(rows * top), side="right").astype(jnp.int32)
    listing = labels.reshape(top, rows).T
    listing = listing[jax.random.permutation(jax.random.fold_in(own, 1), rows)]
    turn = jax.random.randint(jax.random.fold_in(own, 2), (rows, 1), 0, top)
    return jnp.take_along_axis(listing, (jnp.arange(top)[None, :] + turn) % top, axis=1)


def portions_of(number_of, total, most, slope, full):
    loads = [(1 << 20) // math.isqrt(rank ** slope) + 1 for rank in range(1, number_of + 1)]
    largest = most if full else min(most, max(-(-total // number_of), total * loads[0] // sum(loads)))
    least = 1 if total - largest >= number_of - 1 else 0
    given, spare = [largest] + [least] * (number_of - 1), total - largest - least * (number_of - 1)
    while spare > 0:
        movable = [i for i in range(1, number_of) if given[i] < largest] or [i for i in range(1, number_of) if given[i] < most]
        mass, budget = sum([loads[i] for i in movable]), spare
        for i in movable:
            addition = min(most - given[i], max(1, budget * loads[i] // mass), spare)
            given[i] = given[i] + addition
            spare = spare - addition
    return np.array(given)


def scatter_about(own_key, dims, scale, most, shards=(), held_as=jnp.bfloat16):
    entries = jax.random.normal(own_key, dims, jnp.float32) * scale
    if len(shards) > 0:
        entries = block_scale(own_key, dims, shards, -0.22, 0.18) * entries
    return jnp.clip(entries, min=-most, max=most).astype(held_as)


def setup_inputs(seed: int = 0) -> dict:
    key_list = jax.random.split(jax.random.key(seed), 5)
    matrix = scatter_about(key_list[0], (M, M), 1.0, 6.0, ((0, 8), (1, 64)))
    list_x_keys = jax.random.split(jax.random.fold_in(key_list[1], 1), NB // RB)
    list_x_turns = jax.random.permutation(jax.random.fold_in(key_list[1], 3), NB // RB)
    list_x = jax.vmap(lambda own, number: routed_block(jax.random.fold_in(key_list[1], 2), own, number, RB, NB, KX, CAPX, 1))(list_x_keys, list_x_turns).reshape((NB, KX))
    list_sq = different_ones(key_list[2], NB, NB, KSQ, 1920)
    list_out = different_ones(key_list[3], NB, NB, KX, 1280)
    return dict(matrix=matrix, list_x=list_x, list_sq=list_sq, list_out=list_out)


def expand(lists):
    hit = jnp.any(lists[:, :, None] == jnp.arange(NB, dtype=jnp.int32)[None, None, :], axis=1)
    return jnp.broadcast_to(hit[:, None, :, None], (NB, B, NB, B)).reshape(NB * B, NB * B)


def reference(matrix, list_x, list_sq, list_out):
    scale_square = (NB / (KX * KX * B)) ** 0.5
    scale_cube = (NB / (KX * KSQ * B)) ** 0.5
    sparse = jnp.where(expand(list_x), matrix, jnp.zeros_like(matrix))
    product = jnp.dot(sparse, sparse, preferred_element_type=jnp.float32)
    square = jnp.where(expand(list_sq), product * scale_square, jnp.float32(0.0)).astype(jnp.bfloat16)
    cube = jnp.dot(sparse, square, preferred_element_type=jnp.float32) * scale_cube
    result = 1.5 * sparse.astype(jnp.float32) - 0.5 * cube
    return jnp.where(expand(list_out), result, jnp.float32(0.0)).astype(jnp.bfloat16)
```

```python
import functools

import jax
import jax.numpy as jnp
from jax import lax
from jax.experimental import pallas as pl
from jax.experimental.pallas import tpu as pltpu
from jax.sharding import PartitionSpec as P

B = 32
NB = 256
KX = 40
KSQ = 60
CAP = 10
ROWS = 1024
W = 128
BR = ROWS // B
GROUPS = 8
PER = 8
F32 = jnp.float32
BF16 = jnp.bfloat16
MIB = 1 << 20


def lane_hits(lists, base):
    ids = base + lax.broadcasted_iota(jnp.int32, (BR, W), 1) // B
    hit = jnp.zeros((BR, W), F32)
    for t in range(lists.shape[1]):
        hit = jnp.where(lists[:, t : t + 1] == ids, 1.0, hit)
    return hit


def slots_of(hit):
    below = lax.broadcasted_iota(jnp.int32, (BR, BR), 1) < lax.broadcasted_iota(
        jnp.int32, (BR, BR), 0
    )
    rank = jnp.dot(
        jnp.where(below, 1.0, 0.0).astype(BF16), hit.astype(BF16), preferred_element_type=F32
    )
    return jnp.where(hit > 0.0, rank, float(CAP))


def pack_kernel(base_ref, list_ref, tile_ref, pay_ref, left_ref, table_ref):
    lists = list_ref[...]
    hit = lane_hits(lists, base_ref[0])
    slot = slots_of(hit)
    slot_int = slot.astype(jnp.int32)
    packed = [jnp.zeros((B, W), F32) for _ in range(CAP)]
    for i in range(BR):
        block = tile_ref[pl.ds(i * B, B), :].astype(F32)
        row = jnp.broadcast_to(slot_int[i : i + 1, :], (B, W))
        for s in range(min(i + 1, CAP)):
            packed[s] = jnp.where(row == s, block, packed[s])
    for s in range(CAP):
        value = packed[s].astype(BF16)
        pay_ref[pl.ds(s * B, B), :] = value
        left_ref[pl.ds(s * B, B), :] = value
    pay_ref[pl.ds(CAP * B, B), :] = slot.astype(BF16)

    ids = lax.broadcasted_iota(jnp.int32, (BR, NB), 1)
    every = jnp.zeros((BR, NB), F32)
    for t in range(KX):
        every = jnp.where(lists[:, t : t + 1] == ids, 1.0, every)
    table_ref[...] = slots_of(every).astype(jnp.int32) * B


def pack(base, list_x, tile):
    return pl.pallas_call(
        pack_kernel,
        out_shape=(
            jax.ShapeDtypeStruct(((CAP + 1) * B, W), BF16),
            jax.ShapeDtypeStruct((CAP * B, W), BF16),
            jax.ShapeDtypeStruct((BR, NB), jnp.int32),
        ),
        in_specs=[
            pl.BlockSpec(memory_space=pltpu.SMEM),
            pl.BlockSpec(memory_space=pltpu.VMEM),
            pl.BlockSpec(memory_space=pltpu.VMEM),
        ],
        out_specs=(pl.BlockSpec(memory_space=pltpu.VMEM),) * 3,
        compiler_params=pltpu.CompilerParams(vmem_limit_bytes=8 * MIB),
        cost_estimate=pl.CostEstimate(flops=10_000_000, bytes_accessed=500_000, transcendentals=0),
        name="pack",
    )(base, list_x, tile)


def right_kernel(at_ref, base_ref, lx_ref, lsq_ref, lout_ref, *refs):
    pays, (right_ref, masks_ref) = refs[:9], refs[9:]
    masks_ref[0] = lane_hits(lx_ref[...], base_ref[0])
    masks_ref[1] = lane_hits(lsq_ref[...], base_ref[0])
    masks_ref[2] = lane_hits(lout_ref[...], base_ref[0])
    for p in range(GROUPS):
        if p < GROUPS - 1:
            part = [pays[p][pl.ds(s * B, B), :].astype(F32) for s in range(CAP + 1)]
        else:
            half = pays[p].shape[0]
            part = [pays[p][pl.ds(s * B, B), :].astype(F32) for s in range(half // B)]
            part += [pays[p + 1][pl.ds(s * B, B), :].astype(F32) for s in range(CAP + 1 - half // B)]
        slot = part[CAP].astype(jnp.int32)
        g = at_ref[p]
        for i in range(BR):
            row = jnp.broadcast_to(slot[i : i + 1, :], (B, W))
            value = jnp.zeros((B, W), F32)
            for s in range(min(i + 1, CAP)):
                value = jnp.where(row == s, part[s], value)
            right_ref[g, pl.ds(i * B, B), :] = value.astype(BF16)


def right(at, base, list_x, list_sq, list_out, pays):
    smem = pl.BlockSpec(memory_space=pltpu.SMEM)
    vmem = pl.BlockSpec(memory_space=pltpu.VMEM)
    return pl.pallas_call(
        right_kernel,
        out_shape=(
            jax.ShapeDtypeStruct((GROUPS, ROWS, W), BF16),
            jax.ShapeDtypeStruct((3, BR, W), F32),
        ),
        in_specs=[smem, smem] + [vmem] * (3 + len(pays)),
        out_specs=(vmem, vmem),
        compiler_params=pltpu.CompilerParams(vmem_limit_bytes=16 * MIB),
        cost_estimate=pl.CostEstimate(flops=30_000_000, bytes_accessed=3_000_000, transcendentals=0),
        name="right",
    )(at, base, list_x, list_sq, list_out, *pays)


def square_kernel(
    scale, slots_ref, left_ref, right_ref, masks_ref, square_ref, dense_ref, held, dense, acc, in_sems, out_sems
):
    def fetch(g):
        return pltpu.make_async_copy(
            left_ref.at[pl.ds(g * PER, PER)],
            held.at[pl.ds(g * PER, PER), pl.ds(0, CAP * B)],
            in_sems.at[g],
        )

    def put(g):
        return pltpu.make_async_copy(dense.at[g % 2], dense_ref.at[g], out_sems.at[g % 2])

    for g in range(GROUPS):
        fetch(g).start()
    held[:, pl.ds(CAP * B, B), :] = jnp.zeros((GROUPS * PER, B, W), BF16)
    lane = lax.broadcasted_iota(jnp.int32, (B, W), 1)
    for g in range(GROUPS):
        fetch(g).wait()
        if g >= 2:
            put(g - 2).wait()

        @pl.loop(0, BR)
        def _(i):
            for q in range(PER):
                d = g * PER + q
                blocks = [
                    held[d, pl.ds(pl.multiple_of(slots_ref[i, d * 4 + c], B), B), :] for c in range(4)
                ]
                value = jnp.where(
                    lane < 2 * B,
                    jnp.where(lane < B, blocks[0], blocks[1]),
                    jnp.where(lane < 3 * B, blocks[2], blocks[3]),
                )
                dense[g % 2, pl.ds(pl.multiple_of(i * B, B), B), pl.ds(q * W, W)] = value

        put(g).start()
        part = jnp.dot(dense[g % 2], right_ref[g], preferred_element_type=F32)
        acc[...] = part if g == 0 else acc[...] + part
    for i in range(BR):
        keep = jnp.broadcast_to(masks_ref[1, i : i + 1, :], (B, W))
        value = acc[pl.ds(i * B, B), :] * scale
        square_ref[pl.ds(i * B, B), :] = jnp.where(keep > 0.0, value, 0.0).astype(BF16)
    put(GROUPS - 2).wait()
    put(GROUPS - 1).wait()


def square_of(slots, left, right_side, masks):
    scale = (NB / (KX * KX * B)) ** 0.5
    smem = pl.BlockSpec(memory_space=pltpu.SMEM)
    vmem = pl.BlockSpec(memory_space=pltpu.VMEM)
    hbm = pl.BlockSpec(memory_space=pl.ANY)
    return pl.pallas_call(
        functools.partial(square_kernel, scale),
        out_shape=(
            jax.ShapeDtypeStruct((ROWS, W), BF16),
            jax.ShapeDtypeStruct((GROUPS, ROWS, GROUPS * W), BF16),
        ),
        in_specs=[smem, hbm, vmem, vmem],
        out_specs=(vmem, hbm),
        scratch_shapes=[
            pltpu.VMEM((GROUPS * PER, (CAP + 1) * B, W), BF16),
            pltpu.VMEM((2, ROWS, PER * W), BF16),
            pltpu.VMEM((ROWS, W), F32),
            pltpu.SemaphoreType.DMA((GROUPS,)),
            pltpu.SemaphoreType.DMA((2,)),
        ],
        compiler_params=pltpu.CompilerParams(vmem_limit_bytes=32 * MIB),
        cost_estimate=pl.CostEstimate(
            flops=2 * ROWS * GROUPS * ROWS * W, bytes_accessed=24 * MIB, transcendentals=0
        ),
        name="square",
    )(slots, left, right_side, masks)


STEP = 256


def cube_part(at, dense, pieces, acc=None, last=None):
    scale = (NB / (KX * KSQ * B)) ** 0.5
    count = len(pieces)
    spans = [piece[0].shape[0] for piece in pieces]

    def kernel(at_ref, *refs):
        refs = list(refs)
        total = refs.pop(0)[...] if acc is not None else None
        for p in range(count):
            left_ref = refs.pop(0)
            start = 0
            for _ in pieces[p]:
                piece_ref = refs.pop(0)
                size = piece_ref.shape[0]
                term = jnp.dot(
                    left_ref[0, :, pl.ds(start, size)], piece_ref[...], preferred_element_type=F32
                )
                total = term if total is None else total + term
                start += size
        out_ref = refs[-1]
        if last is None:
            out_ref[...] = total
            return
        tile_ref, masks_ref = refs[0], refs[1]
        for k in range(STEP // B):
            rows = pl.ds(k * B, B)
            keep_x = jnp.broadcast_to(masks_ref[0, k : k + 1, :], (B, W))
            keep_out = jnp.broadcast_to(masks_ref[2, k : k + 1, :], (B, W))
            sparse = jnp.where(keep_x > 0.0, tile_ref[rows, :].astype(F32), 0.0)
            cube = total[k * B : (k + 1) * B, :] * scale
            result = 1.5 * sparse - 0.5 * cube
            out_ref[rows, :] = jnp.where(keep_out > 0.0, result, 0.0).astype(BF16)

    operands, specs = [], []
    rows_spec = pl.BlockSpec((STEP, W), lambda i, at_ref: (i, 0))
    if acc is not None:
        operands.append(acc)
        specs.append(rows_spec)
    for p in range(count):
        operands.append(dense)
        specs.append(
            pl.BlockSpec((1, STEP, GROUPS * W), lambda i, at_ref, p=p: (at_ref[p], i, 0))
        )
        for piece in pieces[p]:
            operands.append(piece)
            specs.append(pl.BlockSpec(piece.shape, lambda i, at_ref: (0, 0)))
    if last is not None:
        tile, masks = last
        operands += [tile, masks]
        specs += [rows_spec, pl.BlockSpec((3, STEP // B, W), lambda i, at_ref: (0, i, 0))]
    del spans
    return pl.pallas_call(
        kernel,
        out_shape=jax.ShapeDtypeStruct((ROWS, W), F32 if last is None else BF16),
        grid_spec=pltpu.PrefetchScalarGridSpec(
            num_scalar_prefetch=1,
            grid=(ROWS // STEP,),
            in_specs=specs,
            out_specs=rows_spec,
        ),
        compiler_params=pltpu.CompilerParams(vmem_limit_bytes=24 * MIB),
        cost_estimate=pl.CostEstimate(
            flops=2 * ROWS * ROWS * W * count,
            bytes_accessed=count * 3 * MIB + MIB,
            transcendentals=0,
        ),
        name="cube_last" if last is not None else "cube_part",
    )(at, *operands)


def ring_steps(own, cut):
    ahead = [(i, (i + 1) % GROUPS) for i in range(GROUPS)]
    back = [(i, (i - 1) % GROUPS) for i in range(GROUPS)]
    steps, down, up = [], own, own
    for distance in range(1, GROUPS // 2 + 1):
        if distance == GROUPS // 2:
            down, up = down[:cut], up[cut:]
        down = lax.ppermute(down, "row", ahead)
        up = lax.ppermute(up, "row", back)
        steps.append((down, up))
    return steps


def local(matrix, list_x, list_sq, list_out):
    layers = lax.axis_size("layer")
    tile = lax.axis_index("col") * layers + lax.axis_index("layer")
    base = jnp.reshape(tile * (W // B), (1,)).astype(jnp.int32)
    row = lax.axis_index("row").astype(jnp.int32)
    near = jnp.stack([row, row - 1, row + 1, row - 2, row + 2, row - 3, row + 3, row + 4])
    near = jnp.bitwise_and(near, GROUPS - 1)

    pay, left, slots = pack(base, list_x, matrix)
    lefts = lax.all_gather(left, ("col", "layer"), axis=0, tiled=False)
    hops = ring_steps(pay, 6 * B)
    pays = [pay] + [piece for hop in hops for piece in hop]
    right_side, masks = right(near, base, list_x, list_sq, list_out, pays)

    square, dense = square_of(slots, lefts, right_side, masks)

    hops = ring_steps(square, ROWS // 2)
    acc = cube_part(near[0:1], dense, [(square,)])
    for distance in range(1, GROUPS // 2):
        down, up = hops[distance - 1]
        acc = cube_part(near[2 * distance - 1 : 2 * distance + 1], dense, [(down,), (up,)], acc)
    down, up = hops[-1]
    return cube_part(near[7:8], dense, [(down, up)], acc, (matrix, masks))


def solution(mesh):
    placed = (P("row", ("col", "layer")), P("row", None), P("row", None), P("row", None))
    return jax.shard_map(
        local, mesh=mesh, in_specs=placed, out_specs=P("row", ("col", "layer")), check_vma=False
    )
```

```python
import jax
import jax.numpy as jnp
from jax import lax
from jax.experimental import pallas as pl
from jax.experimental.pallas import tpu as pltpu
from jax.sharding import PartitionSpec as P

B = 32
NB = 256
KX = 40
KSQ = 60
CAP = 10
ROWS = 1024
W = 128
BR = ROWS // B
GROUPS = 8
TILES = 4
HALF = TILES * W
PAY = 576
F32 = jnp.float32
BF16 = jnp.bfloat16
MIB = 1 << 20
SMEM = pl.BlockSpec(memory_space=pltpu.SMEM)
VMEM = pl.BlockSpec(memory_space=pltpu.VMEM)
HBM = pl.BlockSpec(memory_space=pl.ANY)


def params(limit):
    return pltpu.CompilerParams(vmem_limit_bytes=limit * MIB)


def cost(flops, size):
    return pl.CostEstimate(flops=flops, bytes_accessed=size, transcendentals=0)


def copies_in(pairs, sems):
    copies = [pltpu.make_async_copy(a, b, sems.at[k]) for k, (a, b) in enumerate(pairs)]
    for copy in copies:
        copy.start()
    for copy in copies:
        copy.wait()


def lane_hits(lists, base):
    ids = base + lax.broadcasted_iota(jnp.int32, (BR, W), 1) // B
    hit = jnp.zeros((BR, W), F32)
    for t in range(lists.shape[1]):
        hit = jnp.where(lists[:, t : t + 1] == ids, 1.0, hit)
    return hit


def slots_of(hit):
    below = lax.broadcasted_iota(jnp.int32, (BR, BR), 1) < lax.broadcasted_iota(
        jnp.int32, (BR, BR), 0
    )
    rank = jnp.dot(
        jnp.where(below, 1.0, 0.0).astype(BF16), hit.astype(BF16), preferred_element_type=F32
    )
    return jnp.where(hit > 0.0, rank, float(CAP))


def pack_kernel(base_ref, list_hbm, tile_hbm, pay_ref, left_ref, slots_ref, list_ref, tile_ref, sems):
    copies_in([(list_hbm, list_ref), (tile_hbm, tile_ref)], sems)
    lists = list_ref[...]
    hit = lane_hits(lists, base_ref[0])
    slot = slots_of(hit)
    slot_int = slot.astype(jnp.int32)
    packed = [jnp.zeros((B, W), F32) for _ in range(CAP)]
    for i in range(BR):
        block = tile_ref[pl.ds(i * B, B), :].astype(F32)
        row = jnp.broadcast_to(slot_int[i : i + 1, :], (B, W))
        for s in range(min(i + 1, CAP)):
            packed[s] = jnp.where(row == s, block, packed[s])
    for s in range(CAP):
        value = packed[s].astype(BF16)
        pay_ref[pl.ds(s * B, B), :] = value
        left_ref[s] = value
    pay_ref[pl.ds(CAP * B, B), :] = slot.astype(BF16)
    pay_ref[pl.ds((CAP + 1) * B, PAY - (CAP + 1) * B), :] = jnp.zeros(
        (PAY - (CAP + 1) * B, W), BF16
    )

    ids = lax.broadcasted_iota(jnp.int32, (BR, NB), 1)
    every = jnp.zeros((BR, NB), F32)
    for t in range(KX):
        every = jnp.where(lists[:, t : t + 1] == ids, 1.0, every)
    slots_ref[...] = slots_of(every).astype(jnp.int32)


def pack(base, list_x, tile):
    return pl.pallas_call(
        pack_kernel,
        out_shape=(
            jax.ShapeDtypeStruct((PAY, W), BF16),
            jax.ShapeDtypeStruct((CAP, B, W), BF16),
            jax.ShapeDtypeStruct((BR, NB), jnp.int32),
        ),
        in_specs=[SMEM, HBM, HBM],
        out_specs=(VMEM,) * 3,
        scratch_shapes=[
            pltpu.VMEM((BR, KX), jnp.int32),
            pltpu.VMEM((ROWS, W), BF16),
            pltpu.SemaphoreType.DMA((2,)),
        ],
        compiler_params=params(48),
        cost_estimate=cost(10_000_000, 500_000),
        name="pack",
    )(base, list_x, tile)


def order_kernel(table_ref, *refs):
    tiles, out_ref, sems = refs[:TILES], refs[TILES], refs[TILES + 1]
    copies_in([(tile, out_ref.at[table_ref[k]]) for k, tile in enumerate(tiles)], sems)


def order(table, tiles):
    return pl.pallas_call(
        order_kernel,
        out_shape=jax.ShapeDtypeStruct((TILES, CAP, B, W), BF16),
        in_specs=[SMEM] + [HBM] * TILES,
        out_specs=HBM,
        scratch_shapes=[pltpu.SemaphoreType.DMA((TILES,))],
        cost_estimate=cost(0, 700_000),
        name="order",
    )(table, *tiles)


def right_kernel(table_ref, base_ref, *refs):
    lists_hbm, mine_hbm, other_hbm, right_ref, masks_ref = refs[:3], *refs[3:7]
    lists, pays_ref, sems = refs[7:10], refs[10], refs[11]
    rows = pl.ds(0, (CAP + 1) * B)
    pairs = list(zip(lists_hbm, lists))
    pairs += [(ref.at[:, rows], pays_ref.at[k]) for k, ref in enumerate((mine_hbm, other_hbm))]
    copies_in(pairs, sems)
    for k in range(3):
        masks_ref[k] = lane_hits(lists[k][...], base_ref[0])

    @pl.loop(0, 2 * TILES)
    def _(h):
        g, core = table_ref[TILES + 2 * h], table_ref[TILES + 2 * h + 1]
        first = pl.multiple_of(CAP * B + core * (BR // 2), BR // 2)
        for k in range(2):
            part = [pays_ref[k, g, pl.ds(s * B, B), :].astype(F32) for s in range(CAP)]
            slot = pays_ref[k, g, pl.ds(first, BR // 2), :].astype(F32).astype(jnp.int32)
            for t in range(BR // 2):
                row = jnp.broadcast_to(slot[t : t + 1, :], (B, W))
                value = jnp.zeros((B, W), F32)
                for s in range(CAP):
                    value = jnp.where(row == s, part[s], value)
                right_ref[h, pl.ds(t * B, B), pl.ds(k * W, W)] = value.astype(BF16)


def right(table, base, lists, mine, other):
    return pl.pallas_call(
        right_kernel,
        out_shape=(
            jax.ShapeDtypeStruct((2 * TILES, HALF, 2 * W), BF16),
            jax.ShapeDtypeStruct((3, BR, W), F32),
        ),
        in_specs=[SMEM, SMEM] + [HBM] * 5,
        out_specs=(VMEM, VMEM),
        scratch_shapes=[pltpu.VMEM(a.shape, jnp.int32) for a in lists]
        + [
            pltpu.VMEM((2, GROUPS, (CAP + 1) * B, W), BF16),
            pltpu.SemaphoreType.DMA((5,)),
        ],
        compiler_params=params(48),
        cost_estimate=cost(40_000_000, 4 * MIB),
        name="right",
    )(table, base, *lists, mine, other)


def grow(halves, places, table, slots, dense=None, right_side=None, acc=None, split=False):
    count = len(halves)

    def kernel(table_ref, slots_ref, *refs):
        refs = list(refs)
        packed = [refs.pop(0) for _ in halves]
        right_ref = refs.pop(0) if right_side is not None else None
        acc_ref = refs.pop(0) if acc is not None else None
        if dense is not None:
            refs.pop(0)
        held, wide, sems = refs[-3:]
        dense_ref, outs = refs[0], refs[1:-3]

        held[:, :, CAP] = jnp.zeros((count, TILES, B, W), F32)
        lane = lax.broadcasted_iota(jnp.int32, (B, W), 1)
        puts = []
        total = None
        for k in range(count):
            for q in range(TILES):
                for s in range(CAP):
                    held[k, q, s] = packed[k][q, s].astype(F32)
            g, core = table_ref[places[k]], table_ref[places[k] + 1]
            first = (g * 2 + core) * TILES * (W // B)

            @pl.loop(0, BR)
            def _(i):
                for q in range(TILES):
                    part = [held[k, q, slots_ref[i, first + 4 * q + c]] for c in range(4)]
                    value = jnp.where(
                        lane < 2 * B,
                        jnp.where(lane < B, part[0], part[1]),
                        jnp.where(lane < 3 * B, part[2], part[3]),
                    )
                    wide[k, pl.ds(pl.multiple_of(i * B, B), B), pl.ds(q * W, W)] = value.astype(BF16)

            put = pltpu.make_async_copy(wide.at[k], dense_ref.at[g, core], sems.at[k])
            put.start()
            puts.append(put)
            if right_ref is not None:
                at = (places[k] - TILES) // 2
                term = jnp.dot(wide[k], right_ref[at], preferred_element_type=F32)
                total = term if total is None else total + term
        if right_ref is not None:
            if acc_ref is not None:
                total = total + acc_ref[...]
            if split:
                outs[0][...] = total[:, :W]
                outs[1][...] = total[:, W:]
            else:
                outs[0][...] = total
        for put in puts:
            put.wait()

    operands, specs = [table, slots, *halves], [SMEM, SMEM] + [VMEM] * count
    shapes = [jax.ShapeDtypeStruct((GROUPS, 2, ROWS, HALF), BF16)]
    if right_side is not None:
        operands.append(right_side)
        specs.append(VMEM)
        shapes += [jax.ShapeDtypeStruct((ROWS, W), F32)] * 2 if split else [
            jax.ShapeDtypeStruct((ROWS, 2 * W), F32)
        ]
    if acc is not None:
        operands.append(acc)
        specs.append(VMEM)
    aliases = {}
    if dense is not None:
        aliases = {len(operands): 0}
        operands.append(dense)
        specs.append(HBM)
    return pl.pallas_call(
        kernel,
        out_shape=tuple(shapes),
        in_specs=specs,
        out_specs=(HBM,) + (VMEM,) * (len(shapes) - 1),
        scratch_shapes=[
            pltpu.VMEM((count, TILES, CAP + 1, B, W), F32),
            pltpu.VMEM((count, ROWS, HALF), BF16),
            pltpu.SemaphoreType.DMA((count,)),
        ],
        input_output_aliases=aliases,
        compiler_params=params(50),
        cost_estimate=cost(4 * ROWS * HALF * W * count, count * 3 * MIB),
        name="grow" if right_side is not None else "widen",
    )(*operands)


def finish_kernel(mine_ref, other_ref, masks_ref, square_ref):
    scale = (NB / (KX * KX * B)) ** 0.5
    for i in range(BR):
        rows = pl.ds(i * B, B)
        keep = jnp.broadcast_to(masks_ref[1, i : i + 1, :], (B, W))
        value = (mine_ref[rows, :] + other_ref[rows, :]) * scale
        square_ref[rows, :] = jnp.where(keep > 0.0, value, 0.0).astype(BF16)


def finish(mine, other, masks):
    return pl.pallas_call(
        finish_kernel,
        out_shape=jax.ShapeDtypeStruct((ROWS, W), BF16),
        in_specs=[VMEM] * 3,
        out_specs=VMEM,
        cost_estimate=cost(400_000, MIB),
        name="finish",
    )(mine, other, masks)


STEP = 256


def cube_part(places, table, dense, pieces, acc=None, last=None):
    scale = (NB / (KX * KSQ * B)) ** 0.5
    count = len(pieces)

    def kernel(table_ref, *refs):
        refs = list(refs)
        total = refs.pop(0)[...] if acc is not None else None
        for p in range(count):
            left_ref, piece_ref = refs.pop(0), refs.pop(0)
            for core in range(2):
                term = jnp.dot(
                    left_ref[0, core],
                    piece_ref[pl.ds(core * HALF, HALF), :],
                    preferred_element_type=F32,
                )
                total = term if total is None else total + term
        out_ref = refs[-1]
        if last is None:
            out_ref[...] = total
            return
        tile_ref, masks_ref = refs[0], refs[1]
        for k in range(STEP // B):
            rows = pl.ds(k * B, B)
            keep_x = jnp.broadcast_to(masks_ref[0, k : k + 1, :], (B, W))
            keep_out = jnp.broadcast_to(masks_ref[2, k : k + 1, :], (B, W))
            sparse = jnp.where(keep_x > 0.0, tile_ref[rows, :].astype(F32), 0.0)
            cube = total[k * B : (k + 1) * B, :] * scale
            result = 1.5 * sparse - 0.5 * cube
            out_ref[rows, :] = jnp.where(keep_out > 0.0, result, 0.0).astype(BF16)

    operands, specs = [], []
    rows_spec = pl.BlockSpec((STEP, W), lambda i, table_ref: (i, 0))
    if acc is not None:
        operands.append(acc)
        specs.append(rows_spec)
    for p in range(count):
        operands += [dense, pieces[p]]
        if last is None:
            place = lambda i, table_ref, p=p: (table_ref[places[p]], 0, i, 0)
        else:
            place = lambda i, table_ref: (0, 0, i, 0)
        specs.append(pl.BlockSpec((1, 2, STEP, HALF), place))
        specs.append(pl.BlockSpec((ROWS, W), lambda i, table_ref: (0, 0)))
    if last is not None:
        tile, masks = last
        operands += [tile, masks]
        specs += [rows_spec, pl.BlockSpec((3, STEP // B, W), lambda i, table_ref: (0, i, 0))]
    return pl.pallas_call(
        kernel,
        out_shape=jax.ShapeDtypeStruct((ROWS, W), F32 if last is None else BF16),
        grid_spec=pltpu.PrefetchScalarGridSpec(
            num_scalar_prefetch=1,
            grid=(ROWS // STEP,),
            in_specs=specs,
            out_specs=rows_spec,
        ),
        compiler_params=params(50 if last is None else 16),
        cost_estimate=cost(2 * ROWS * ROWS * W * count, count * 3 * MIB + MIB),
        name="cube_last" if last is not None else "cube_part",
    )(table, *operands)


def local(matrix, list_x, list_sq, list_out):
    layers = lax.axis_size("layer")
    col = lax.axis_index("col").astype(jnp.int32)
    row = lax.axis_index("row").astype(jnp.int32)
    layer = lax.axis_index("layer").astype(jnp.int32)
    y, core = col // 2, col % 2
    sign = 1 - 2 * core
    base = jnp.reshape((col * layers + layer) * (W // B), (1,))

    def group(at, distance):
        return jnp.bitwise_and(at + sign * distance, GROUPS - 1)

    table = [jnp.bitwise_and(layer + d, TILES - 1) for d in (0, -1, 1, 2)]
    for turn, own in ((-1, core), (1, 1 - core)):
        for d, which in ((0, own), (1, own), (1, 1 - own), (2, own), (2, 1 - own), (3, own), (3, 1 - own), (4, own)):
            table += [group(y, turn * d), which]
    table += [group(row, d) for d in (0, -1, 1, -2, 2, -3, 3, 4)]
    table = jnp.stack(table)
    mine_at, other_at, z_at = 4, 20, 36

    cols = 2 * GROUPS
    swap = [(c, c ^ 1) for c in range(cols)]
    turn_y = [(c, (c + (2 if c % 2 == 0 else -2)) % cols) for c in range(cols)]
    turn_z = [
        (r * cols + c, (r + (1 if c % 2 == 0 else -1)) % GROUPS * cols + c)
        for r in range(GROUPS)
        for c in range(cols)
    ]

    def along_x(piece, step):
        return lax.ppermute(piece, "layer", [(x, (x + step) % layers) for x in range(layers)])

    def along_y(piece):
        return lax.ppermute(piece, "col", turn_y)

    def along_z(piece):
        return lax.ppermute(piece, ("row", "col"), turn_z)

    def across(piece):
        return lax.ppermute(piece, "col", swap)

    def after(piece, *done):
        return lax.optimization_barrier((piece, *done))[0]

    pay, left, slots = pack(base, list_x, matrix)
    pays = lax.all_gather(pay, "row", axis=0, tiled=False)
    a0 = order(table, [left, along_x(left, 1), along_x(left, -1), along_x(left, 2)])
    b0 = across(a0)

    def places(start, *which):
        return [start + 2 * k for k in which]

    a1, b1 = along_y(a0), along_y(b0)
    a2, b2 = along_y(a1), along_y(b1)
    a3, b3 = along_y(a2), along_y(b2)
    pays = after(pays, a2)
    right_side, masks = right(table, base, (list_x, list_sq, list_out), pays, across(pays))
    dense, acc = grow([a0, a1, b1], places(mine_at, 0, 1, 2), table, slots, None, right_side)
    a4 = along_y(after(a3, acc))
    dense, acc = grow([a2, b2], places(mine_at, 3, 4), table, slots, dense, right_side, acc)
    dense, acc = grow([a3, b3], places(mine_at, 5, 6), table, slots, dense, right_side, acc)
    dense, mine, other = grow(
        [a4], places(mine_at, 7), table, slots, dense, right_side, acc, split=True
    )
    square = finish(mine, across(other), masks)

    theirs = jnp.concatenate([a1, b1, a2, b2, a3, b3, a4], axis=0)
    theirs = across(after(theirs, other))
    c0, d0 = square, across(square)
    c1, d1 = along_z(c0), along_z(d0)
    (dense,) = grow(
        [b0] + [theirs[k * TILES : (k + 1) * TILES] for k in range(7)],
        places(other_at, *range(8)),
        table,
        slots,
        dense,
    )
    acc = cube_part([z_at], table, dense, [c0])
    c1, d1 = lax.optimization_barrier((c1, d1, acc))[:2]
    c2, d2 = along_z(c1), along_z(d1)
    acc = cube_part([z_at + 1, z_at + 2], table, dense, [c1, across(d1)], acc)
    c2, d2 = lax.optimization_barrier((c2, d2, acc))[:2]
    c3, d3 = along_z(c2), along_z(d2)
    acc = cube_part([z_at + 3, z_at + 4], table, dense, [c2, across(d2)], acc)
    c4 = along_z(after(c3, acc))
    acc = cube_part([z_at + 5, z_at + 6], table, dense, [c3, across(d3)], acc)
    far = lax.dynamic_slice_in_dim(dense, group(row, 4), 1, 0)
    return cube_part([0], table, far, [c4], acc, (matrix, masks))


def solution(mesh):
    placed = (P("row", ("col", "layer")), P("row", None), P("row", None), P("row", None))
    return jax.shard_map(
        local, mesh=mesh, in_specs=placed, out_specs=P("row", ("col", "layer")), check_vma=False
    )
```

```python
import jax
import jax.numpy as jnp
from jax import lax
from jax.experimental import pallas as pl
from jax.experimental.pallas import tpu as pltpu
from jax.sharding import PartitionSpec as P

B = 32
NB = 256
KX = 40
KSQ = 60
CAP = 10
ROWS = 1024
W = 128
BR = ROWS // B
GROUPS = 8
TILES = 4
HALF = TILES * W
PAY = 576
F32 = jnp.float32
BF16 = jnp.bfloat16
MIB = 1 << 20
SMEM = pl.BlockSpec(memory_space=pltpu.SMEM)
VMEM = pl.BlockSpec(memory_space=pltpu.VMEM)
HBM = pl.BlockSpec(memory_space=pl.ANY)


def params(limit):
    return pltpu.CompilerParams(vmem_limit_bytes=limit * MIB)


def cost(flops, size):
    return pl.CostEstimate(flops=flops, bytes_accessed=size, transcendentals=0)


def copies_in(pairs, sems):
    copies = [pltpu.make_async_copy(a, b, sems.at[k]) for k, (a, b) in enumerate(pairs)]
    for copy in copies:
        copy.start()
    for copy in copies:
        copy.wait()


def lane_hits(lists, base):
    ids = base + lax.broadcasted_iota(jnp.int32, (BR, W), 1) // B
    hit = jnp.zeros((BR, W), F32)
    for t in range(lists.shape[1]):
        hit = jnp.where(lists[:, t : t + 1] == ids, 1.0, hit)
    return hit


def slots_of(hit):
    below = lax.broadcasted_iota(jnp.int32, (BR, BR), 1) < lax.broadcasted_iota(
        jnp.int32, (BR, BR), 0
    )
    rank = jnp.dot(
        jnp.where(below, 1.0, 0.0).astype(BF16), hit.astype(BF16), preferred_element_type=F32
    )
    return jnp.where(hit > 0.0, rank, float(CAP))


def pack_kernel(base_ref, list_hbm, tile_hbm, pay_ref, left_ref, places_ref, list_ref, tile_ref, sems):
    copies_in([(list_hbm, list_ref), (tile_hbm, tile_ref)], sems)
    lists = list_ref[...]
    hit = lane_hits(lists, base_ref[0])
    slot = slots_of(hit)
    slot_int = slot.astype(jnp.int32)
    packed = [jnp.zeros((B, W), F32) for _ in range(CAP)]
    for i in range(BR):
        block = tile_ref[pl.ds(i * B, B), :].astype(F32)
        row = jnp.broadcast_to(slot_int[i : i + 1, :], (B, W))
        for s in range(min(i + 1, CAP)):
            packed[s] = jnp.where(row == s, block, packed[s])
    for s in range(CAP):
        value = packed[s].astype(BF16)
        pay_ref[pl.ds(s * B, B), :] = value
        for x in range(TILES):
            left_ref[x, s] = value
    pay_ref[pl.ds(CAP * B, B), :] = slot.astype(BF16)
    pay_ref[pl.ds((CAP + 1) * B, PAY - (CAP + 1) * B), :] = jnp.zeros(
        (PAY - (CAP + 1) * B, W), BF16
    )

    ids = lax.broadcasted_iota(jnp.int32, (BR, NB), 1)
    every = jnp.zeros((BR, NB), F32)
    for t in range(KX):
        every = jnp.where(lists[:, t : t + 1] == ids, 1.0, every)
    slot = slots_of(every)
    rows = lax.broadcasted_iota(jnp.int32, (BR, NB), 0).astype(F32) - BR
    for s in range(CAP):
        at = jnp.sum(jnp.where(slot == s, rows, 0.0), axis=0, keepdims=True) + BR
        places_ref[pl.ds(s, 1), :] = at.astype(jnp.int32)


def pack(base, list_x, tile):
    return pl.pallas_call(
        pack_kernel,
        out_shape=(
            jax.ShapeDtypeStruct((PAY, W), BF16),
            jax.ShapeDtypeStruct((TILES, CAP, B, W), BF16),
            jax.ShapeDtypeStruct((CAP, NB), jnp.int32),
        ),
        in_specs=[SMEM, HBM, HBM],
        out_specs=(VMEM,) * 3,
        scratch_shapes=[
            pltpu.VMEM((BR, KX), jnp.int32),
            pltpu.VMEM((ROWS, W), BF16),
            pltpu.SemaphoreType.DMA((2,)),
        ],
        compiler_params=params(48),
        cost_estimate=cost(10_000_000, 500_000),
        name="pack",
    )(base, list_x, tile)


def right_kernel(table_ref, base_ref, *refs):
    lists_hbm, mine_hbm, other_hbm, right_ref, masks_ref = refs[:3], *refs[3:7]
    lists, pays_ref, sems = refs[7:10], refs[10], refs[11]
    rows = pl.ds(0, (CAP + 1) * B)
    pairs = list(zip(lists_hbm, lists))
    pairs += [(ref.at[:, rows], pays_ref.at[k]) for k, ref in enumerate((mine_hbm, other_hbm))]
    copies_in(pairs, sems)
    for k in range(3):
        masks_ref[k] = lane_hits(lists[k][...], base_ref[0])

    @pl.loop(0, 2 * TILES)
    def _(h):
        g, core = table_ref[2 * h], table_ref[2 * h + 1]
        first = pl.multiple_of(CAP * B + core * (BR // 2), BR // 2)
        for k in range(2):
            part = [pays_ref[k, g, pl.ds(s * B, B), :].astype(F32) for s in range(CAP)]
            slot = pays_ref[k, g, pl.ds(first, BR // 2), :].astype(F32).astype(jnp.int32)
            for t in range(BR // 2):
                row = jnp.broadcast_to(slot[t : t + 1, :], (B, W))
                value = jnp.zeros((B, W), F32)
                for s in range(CAP):
                    value = jnp.where(row == s, part[s], value)
                right_ref[h, pl.ds(t * B, B), pl.ds(k * W, W)] = value.astype(BF16)


def right(table, base, lists, mine, other):
    return pl.pallas_call(
        right_kernel,
        out_shape=(
            jax.ShapeDtypeStruct((2 * TILES, HALF, 2 * W), BF16),
            jax.ShapeDtypeStruct((3, BR, W), F32),
        ),
        in_specs=[SMEM, SMEM] + [HBM] * 5,
        out_specs=(VMEM, VMEM),
        scratch_shapes=[pltpu.VMEM(a.shape, jnp.int32) for a in lists]
        + [
            pltpu.VMEM((2, GROUPS, (CAP + 1) * B, W), BF16),
            pltpu.SemaphoreType.DMA((5,)),
        ],
        compiler_params=params(48),
        cost_estimate=cost(40_000_000, 4 * MIB),
        name="right",
    )(table, base, *lists, mine, other)


def widen(first, halves, table, places, dense=None):
    count = len(halves)

    def kernel(table_ref, places_ref, *refs):
        packed, refs = refs[:count], refs[count:]
        dense_ref, rows, wide, sems = refs if dense is None else refs[1:]
        lane = lax.broadcasted_iota(jnp.int32, (B, W), 1) // B
        masks = [lane == c for c in range(W // B)]
        puts = []
        for k in range(count):
            g, core = table_ref[2 * (first + k)], table_ref[2 * (first + k) + 1]
            start = (g * 2 + core) * HALF // B
            for q in range(TILES):
                rows[q, pl.ds(0, BR)] = jnp.zeros((BR, B, W), F32)
            for q in range(TILES):
                for s in range(CAP):
                    block = packed[k][q, s].astype(F32)
                    for c in range(W // B):
                        row = places_ref[s, start + q * (W // B) + c]
                        pltpu.store(rows.at[q, row], block, mask=masks[c])
            for q in range(TILES):
                for i in range(BR):
                    wide[k, pl.ds(i * B, B), pl.ds(q * W, W)] = rows[q, i].astype(BF16)
            put = pltpu.make_async_copy(wide.at[k], dense_ref.at[first + k], sems.at[k])
            put.start()
            puts.append(put)
        for put in puts:
            put.wait()

    operands, specs = [table, places, *halves], [SMEM, SMEM] + [VMEM] * count
    aliases = {}
    if dense is not None:
        aliases = {len(operands): 0}
        operands.append(dense)
        specs.append(HBM)
    return pl.pallas_call(
        kernel,
        out_shape=jax.ShapeDtypeStruct((2 * TILES, ROWS, HALF), BF16),
        in_specs=specs,
        out_specs=HBM,
        scratch_shapes=[
            pltpu.VMEM((TILES, BR + 1, B, W), F32),
            pltpu.VMEM((count, ROWS, HALF), BF16),
            pltpu.SemaphoreType.DMA((count,)),
        ],
        input_output_aliases=aliases,
        compiler_params=params(50),
        cost_estimate=cost(4 * ROWS * HALF * W * count, count * 3 * MIB),
        name="widen",
    )(*operands)


STEP = 256


def product_kernel(dense_ref, right_ref, mine_ref, other_ref):
    total = jnp.dot(dense_ref[0], right_ref[0], preferred_element_type=F32)
    for k in range(1, 2 * TILES):
        total += jnp.dot(dense_ref[k], right_ref[k], preferred_element_type=F32)
    mine_ref[...] = total[:, :W]
    other_ref[...] = total[:, W:]


def product(dense, right_side):
    part = pl.BlockSpec((STEP, W), lambda i: (i, 0))
    return pl.pallas_call(
        product_kernel,
        out_shape=(jax.ShapeDtypeStruct((ROWS, W), F32),) * 2,
        grid=(ROWS // STEP,),
        in_specs=[
            pl.BlockSpec((2 * TILES, STEP, HALF), lambda i: (0, i, 0)),
            pl.BlockSpec((2 * TILES, HALF, 2 * W), lambda i: (0, 0, 0)),
        ],
        out_specs=(part, part),
        compiler_params=params(50),
        cost_estimate=cost(8 * ROWS * ROWS * W * 2, 12 * MIB),
        name="product",
    )(dense, right_side)


def finish_kernel(mine_ref, other_ref, masks_ref, square_ref):
    scale = (NB / (KX * KX * B)) ** 0.5
    for i in range(BR):
        rows = pl.ds(i * B, B)
        keep = jnp.broadcast_to(masks_ref[1, i : i + 1, :], (B, W))
        value = (mine_ref[rows, :] + other_ref[rows, :]) * scale
        square_ref[rows, :] = jnp.where(keep > 0.0, value, 0.0).astype(BF16)


def finish(mine, other, masks):
    return pl.pallas_call(
        finish_kernel,
        out_shape=jax.ShapeDtypeStruct((ROWS, W), BF16),
        in_specs=[VMEM] * 3,
        out_specs=VMEM,
        cost_estimate=cost(400_000, MIB),
        name="finish",
    )(mine, other, masks)


def cube_part(steps, table, own, other, pieces, acc=None, last=None):
    scale = (NB / (KX * KSQ * B)) ** 0.5
    count = len(pieces)

    def kernel(table_ref, own_ref, other_ref, *refs):
        refs = list(refs)
        pieces_refs = [[refs.pop(0) for _ in piece] for piece in pieces]
        acc_ref = refs.pop(0) if acc is not None else None
        tile_ref, masks_ref = (refs.pop(0), refs.pop(0)) if last is not None else (None, None)
        out_ref, held, sems = refs
        y, row, core = (table_ref[4 * TILES + k] for k in range(3))
        for h in range(2 * count):
            d = jnp.bitwise_and((y - row - steps[h // 2]) * (1 - 2 * core), GROUPS - 1)
            same = core == h % 2
            ours = jnp.logical_or(jnp.logical_and(same, d <= 4), jnp.logical_and(d > 0, d < 4))
            d = jnp.where(d > 4, GROUPS - d, d)
            at = jnp.where(d == 0, 0, 2 * d - jnp.where(same == ours, 1, 0))
            at = jnp.where(d == 4, 2 * TILES - 1, at)
            at = jnp.where(ours, at, at + 2 * TILES)

            @pl.when(at < 2 * TILES)
            def _():
                pltpu.make_async_copy(own_ref.at[at], held.at[h], sems.at[h]).start()

            @pl.when(at >= 2 * TILES)
            def _():
                pltpu.make_async_copy(other_ref.at[at - 2 * TILES], held.at[h], sems.at[h]).start()

        total = None if acc_ref is None else acc_ref[...]
        for h in range(2 * count):
            pltpu.make_async_copy(own_ref.at[0], held.at[h], sems.at[h]).wait()
            refs_of = pieces_refs[h // 2]
            if len(refs_of) == 2:
                piece = refs_of[h % 2][...]
            else:
                piece = refs_of[0][pl.ds(h % 2 * HALF, HALF), :]
            term = jnp.dot(held[h], piece, preferred_element_type=F32)
            total = term if total is None else total + term
        if last is None:
            out_ref[...] = total
            return
        for k in range(BR):
            rows = pl.ds(k * B, B)
            keep_x = jnp.broadcast_to(masks_ref[0, k : k + 1, :], (B, W))
            keep_out = jnp.broadcast_to(masks_ref[2, k : k + 1, :], (B, W))
            sparse = jnp.where(keep_x > 0.0, tile_ref[rows, :].astype(F32), 0.0)
            cube = total[k * B : (k + 1) * B, :] * scale
            result = 1.5 * sparse - 0.5 * cube
            out_ref[rows, :] = jnp.where(keep_out > 0.0, result, 0.0).astype(BF16)

    operands = [table, own, other] + [array for piece in pieces for array in piece]
    if acc is not None:
        operands.append(acc)
    if last is not None:
        operands += last
    return pl.pallas_call(
        kernel,
        out_shape=jax.ShapeDtypeStruct((ROWS, W), F32 if last is None else BF16),
        in_specs=[SMEM, HBM, HBM] + [VMEM] * (len(operands) - 3),
        out_specs=VMEM,
        scratch_shapes=[
            pltpu.VMEM((2 * count, ROWS, HALF), BF16),
            pltpu.SemaphoreType.DMA((2 * count,)),
        ],
        compiler_params=params(50),
        cost_estimate=cost(2 * ROWS * ROWS * W * count, count * 3 * MIB + MIB),
        name="cube_last" if last is not None else "cube_part",
    )(*operands)


def local(matrix, list_x, list_sq, list_out):
    layers = lax.axis_size("layer")
    col = lax.axis_index("col").astype(jnp.int32)
    row = lax.axis_index("row").astype(jnp.int32)
    layer = lax.axis_index("layer").astype(jnp.int32)
    y, core = col // 2, col % 2
    sign = 1 - 2 * core
    base = jnp.reshape((col * layers + layer) * (W // B), (1,))

    brought = [(0, 1), (1, 1), (1, 0), (2, 1), (2, 0), (3, 1), (3, 0), (4, 1)]
    table = []
    for d, same in brought:
        table += [jnp.bitwise_and(y - sign * d, GROUPS - 1), core if same else 1 - core]
    table = jnp.stack(table + [y, row, core])
    cols = 2 * GROUPS
    swap = [(c, c ^ 1) for c in range(cols)]
    turn_y = [(c, (c + (2 if c % 2 == 0 else -2)) % cols) for c in range(cols)]

    def along_y(piece):
        return lax.ppermute(piece, "col", turn_y)

    def along_z(piece, step):
        return lax.ppermute(piece, "row", [(r, (r + step) % GROUPS) for r in range(GROUPS)])

    def across(piece):
        return lax.ppermute(piece, "col", swap)

    def after(piece, *done):
        return lax.optimization_barrier((piece, *done))[0]

    pay, left, places = pack(base, list_x, matrix)
    pays = lax.all_gather(pay, "row", axis=0, tiled=False)
    a0 = lax.all_to_all(left, "layer", 0, 0, tiled=True)
    b0 = across(a0)
    a1, b1 = along_y(a0), along_y(b0)
    dense = widen(0, [a0], table, places)
    a2, b2 = along_y(after(a1, dense)), along_y(b1)
    dense = widen(1, [a1, b1], table, places, dense)
    a3, b3 = along_y(after(a2, dense)), along_y(b2)
    dense = widen(3, [a2, b2], table, places, dense)
    a4 = along_y(after(a3, dense))
    dense = widen(5, [a3, b3], table, places, dense)
    pays = after(pays, dense)
    right_side, masks = right(table, base, (list_x, list_sq, list_out), pays, across(pays))
    dense = widen(7, [a4], table, places, dense)
    mine, other = product(dense, right_side)
    square = finish(mine, across(other), masks)

    def cubed(distance, pieces, *more):
        steps = [distance] if distance in (0, GROUPS // 2) else [-distance, distance]
        return cube_part(steps, table, dense, theirs, pieces, *more)

    down, up = along_z(square, 1), along_z(square, -1)
    theirs = across(after(dense, square))
    acc = cubed(0, [(square,)])
    down2, up2 = along_z(down, 1), along_z(up, -1)
    acc = cubed(1, [(down,), (up,)], acc)
    down3, up3 = along_z(after(down2, acc), 1), along_z(up2, -1)
    acc = cubed(2, [(down2,), (up2,)], acc)
    down4, up4 = along_z(after(down3[:HALF], acc), 1), along_z(up3[HALF:], -1)
    acc = cubed(3, [(down3,), (up3,)], acc)
    return cubed(4, [(down4, up4)], acc, (matrix, masks))


def solution(mesh):
    placed = (P("row", ("col", "layer")), P("row", None), P("row", None), P("row", None))
    return jax.shard_map(
        local, mesh=mesh, in_specs=placed, out_specs=P("row", ("col", "layer")), check_vma=False
    )
```

```python
import jax
import jax.numpy as jnp
from jax import lax
from jax.experimental import pallas as pl
from jax.experimental.pallas import tpu as pltpu
from jax.sharding import PartitionSpec as P

B = 32
NB = 256
KX = 40
KSQ = 60
CAP = 10
ROWS = 1024
W = 128
BR = ROWS // B
GROUPS = 8
TILES = 4
HALF = TILES * W
PAY = 576
FIRST, REST = 5, 3
F32 = jnp.float32
BF16 = jnp.bfloat16
MIB = 1 << 20
SMEM = pl.BlockSpec(memory_space=pltpu.SMEM)
VMEM = pl.BlockSpec(memory_space=pltpu.VMEM)
HBM = pl.BlockSpec(memory_space=pltpu.HBM)


def params(limit):
    return pltpu.CompilerParams(vmem_limit_bytes=limit * MIB)


COST = pl.CostEstimate(flops=1, bytes_accessed=1, transcendentals=0)


def copies_in(pairs, sems):
    copies = [pltpu.make_async_copy(a, b, sems.at[k]) for k, (a, b) in enumerate(pairs)]
    for copy in copies:
        copy.start()
    for copy in copies:
        copy.wait()


def lane_hits(lists, base):
    ids = base + lax.broadcasted_iota(jnp.int32, (BR, W), 1) // B
    hit = jnp.zeros((BR, W), F32)
    for t in range(lists.shape[1]):
        hit = jnp.where(lists[:, t : t + 1] == ids, 1.0, hit)
    return hit


def slots_of(hit):
    below = lax.broadcasted_iota(jnp.int32, (BR, BR), 1) < lax.broadcasted_iota(
        jnp.int32, (BR, BR), 0
    )
    rank = jnp.dot(
        jnp.where(below, 1.0, 0.0).astype(BF16), hit.astype(BF16), preferred_element_type=F32
    )
    return jnp.where(hit > 0.0, rank, float(CAP))


def pack_kernel(base_ref, list_hbm, tile_hbm, pay_ref, left_ref, places_ref, list_ref, tile_ref, sems):
    copies_in([(list_hbm, list_ref), (tile_hbm, tile_ref)], sems)
    lists = list_ref[...]
    hit = lane_hits(lists, base_ref[0])
    slot = slots_of(hit)
    slot_int = slot.astype(jnp.int32)
    packed = [jnp.zeros((B, W), F32) for _ in range(CAP)]
    for i in range(BR):
        block = tile_ref[pl.ds(i * B, B), :].astype(F32)
        row = jnp.broadcast_to(slot_int[i : i + 1, :], (B, W))
        for s in range(min(i + 1, CAP)):
            packed[s] = jnp.where(row == s, block, packed[s])
    for s in range(CAP):
        value = packed[s].astype(BF16)
        pay_ref[pl.ds(s * B, B), :] = value
        for x in range(TILES):
            left_ref[x, s] = value
    pay_ref[pl.ds(CAP * B, B), :] = slot.astype(BF16)
    pay_ref[pl.ds((CAP + 1) * B, PAY - (CAP + 1) * B), :] = jnp.zeros(
        (PAY - (CAP + 1) * B, W), BF16
    )

    ids = lax.broadcasted_iota(jnp.int32, (BR, NB), 1)
    every = jnp.zeros((BR, NB), F32)
    for t in range(KX):
        every = jnp.where(lists[:, t : t + 1] == ids, 1.0, every)
    slot = slots_of(every)
    rows = lax.broadcasted_iota(jnp.int32, (BR, NB), 0).astype(F32) - BR
    for s in range(CAP):
        at = jnp.sum(jnp.where(slot == s, rows, 0.0), axis=0, keepdims=True) + BR
        places_ref[pl.ds(s, 1), :] = at.astype(jnp.int32)


def pack(base, list_x, tile):
    return pl.pallas_call(
        pack_kernel,
        out_shape=(
            jax.ShapeDtypeStruct((PAY, W), BF16),
            jax.ShapeDtypeStruct((TILES, CAP, B, W), BF16),
            jax.ShapeDtypeStruct((CAP, NB), jnp.int32),
        ),
        in_specs=[SMEM, HBM, HBM],
        out_specs=(VMEM,) * 3,
        scratch_shapes=[
            pltpu.VMEM((BR, KX), jnp.int32),
            pltpu.VMEM((ROWS, W), BF16),
            pltpu.SemaphoreType.DMA((2,)),
        ],
        compiler_params=params(48),
        cost_estimate=COST,
        name="pack",
    )(base, list_x, tile)


def right_kernel(table_ref, base_ref, *refs):
    lists_hbm, mine_hbm, other_hbm, right_ref, masks_ref = refs[:3], *refs[3:7]
    lists, pays_ref, sems = refs[7:10], refs[10], refs[11]
    rows = pl.ds(0, (CAP + 1) * B)
    pairs = list(zip(lists_hbm, lists))
    pairs += [(ref.at[:, rows], pays_ref.at[k]) for k, ref in enumerate((mine_hbm, other_hbm))]
    copies_in(pairs, sems)
    for k, (which, owner) in enumerate(((0, 0), (2, 0), (1, 0), (1, 1))):
        masks_ref[k] = lane_hits(lists[which][...], base_ref[owner])

    @pl.loop(0, 2 * TILES)
    def _(h):
        g, core = table_ref[2 * h], table_ref[2 * h + 1]
        first = pl.multiple_of(CAP * B + core * (BR // 2), BR // 2)
        for k in range(2):
            part = [pays_ref[k, g, pl.ds(s * B, B), :].astype(F32) for s in range(CAP)]
            slot = pays_ref[k, g, pl.ds(first, BR // 2), :].astype(F32).astype(jnp.int32)
            for t in range(BR // 2):
                row = jnp.broadcast_to(slot[t : t + 1, :], (B, W))
                value = jnp.zeros((B, W), F32)
                for s in range(CAP):
                    value = jnp.where(row == s, part[s], value)
                right_ref[h, pl.ds(t * B, B), pl.ds(k * W, W)] = value.astype(BF16)


def right(table, base, lists, mine, other):
    return pl.pallas_call(
        right_kernel,
        out_shape=(
            jax.ShapeDtypeStruct((2 * TILES, HALF, 2 * W), BF16),
            jax.ShapeDtypeStruct((4, BR, W), F32),
        ),
        in_specs=[SMEM, SMEM] + [HBM] * 5,
        out_specs=(VMEM, VMEM),
        scratch_shapes=[pltpu.VMEM(a.shape, jnp.int32) for a in lists]
        + [
            pltpu.VMEM((2, GROUPS, (CAP + 1) * B, W), BF16),
            pltpu.SemaphoreType.DMA((5,)),
        ],
        compiler_params=params(48),
        cost_estimate=COST,
        name="right",
    )(table, base, *lists, mine, other)


def unpack(packed_ref, start, places_ref, rows, wide):
    lane = lax.broadcasted_iota(jnp.int32, (B, W), 1) // B
    masks = [lane == c for c in range(W // B)]
    for q in range(TILES):
        rows[q, pl.ds(0, BR)] = jnp.zeros((BR, B, W), F32)
    for q in range(TILES):
        for s in range(CAP):
            block = packed_ref[q, s].astype(F32)
            for c in range(W // B):
                row = places_ref[s, start + q * (W // B) + c]
                pltpu.store(rows.at[q, row], block, mask=masks[c])
    for q in range(TILES):
        for i in range(BR):
            wide[pl.ds(i * B, B), pl.ds(q * W, W)] = rows[q, i].astype(BF16)


def half_start(table_ref, k):
    return (table_ref[2 * k] * 2 + table_ref[2 * k + 1]) * (HALF // B)


def widen(first, halves, table, places, dense=None):
    count = len(halves)

    def kernel(table_ref, places_ref, *refs):
        packed, refs = refs[:count], refs[count:]
        dense_ref, rows, wide, sems = refs if dense is None else refs[1:]
        puts = []
        for k in range(count):
            unpack(packed[k], half_start(table_ref, first + k), places_ref, rows, wide.at[k])
            put = pltpu.make_async_copy(wide.at[k], dense_ref.at[first + k], sems.at[k])
            put.start()
            puts.append(put)
        for put in puts:
            put.wait()

    operands, specs = [table, places, *halves], [SMEM, SMEM] + [VMEM] * count
    aliases = {}
    if dense is not None:
        aliases = {len(operands): 0}
        operands.append(dense)
        specs.append(HBM)
    return pl.pallas_call(
        kernel,
        out_shape=jax.ShapeDtypeStruct((FIRST, ROWS, HALF), BF16),
        in_specs=specs,
        out_specs=HBM,
        scratch_shapes=[
            pltpu.VMEM((TILES, BR + 1, B, W), F32),
            pltpu.VMEM((count, ROWS, HALF), BF16),
            pltpu.SemaphoreType.DMA((count,)),
        ],
        input_output_aliases=aliases,
        compiler_params=params(50),
        cost_estimate=COST,
        name="widen",
    )(*operands)


def product(halves, table, places, dense, right_side):
    count = FIRST + len(halves)

    def kernel(table_ref, places_ref, *refs):
        packed, refs = refs[: len(halves)], refs[len(halves) :]
        right_ref, dense_in, dense_ref, sum_ref, rows, wide, in_sems, out_sems = refs
        fetches = [
            pltpu.make_async_copy(dense_in.at[k], wide.at[k], in_sems.at[k]) for k in range(FIRST)
        ]
        for fetch in fetches:
            fetch.start()
        puts = []
        for k in range(len(halves)):
            at = FIRST + k
            unpack(packed[k], half_start(table_ref, at), places_ref, rows, wide.at[at])
            put = pltpu.make_async_copy(wide.at[at], dense_ref.at[k], out_sems.at[k])
            put.start()
            puts.append(put)
        for fetch in fetches:
            fetch.wait()

        @pl.loop(0, ROWS // STEP)
        def _(i):
            part = pl.ds(pl.multiple_of(i * STEP, STEP), STEP)
            total = jnp.dot(wide[0, part, :], right_ref[0], preferred_element_type=F32)
            for k in range(1, count):
                total += jnp.dot(wide[k, part, :], right_ref[k], preferred_element_type=F32)
            sum_ref[part, :] = total

        for put in puts:
            put.wait()

    return pl.pallas_call(
        kernel,
        out_shape=(
            jax.ShapeDtypeStruct((REST, ROWS, HALF), BF16),
            jax.ShapeDtypeStruct((ROWS, 2 * W), F32),
        ),
        in_specs=[SMEM, SMEM] + [VMEM] * (len(halves) + 1) + [HBM],
        out_specs=(HBM, VMEM),
        scratch_shapes=[
            pltpu.VMEM((TILES, BR + 1, B, W), F32),
            pltpu.VMEM((count, ROWS, HALF), BF16),
            pltpu.SemaphoreType.DMA((FIRST,)),
            pltpu.SemaphoreType.DMA((len(halves),)),
        ],
        compiler_params=params(50),
        cost_estimate=COST,
        name="product",
    )(table, places, *halves, right_side, dense)


STEP = 256


def close_kernel(
    table_ref, places_ref, packed_ref, right_ref, sum_ref, dense_in, dense_ref, out_ref, rows, wide, sem
):
    last = FIRST + REST - 1
    unpack(packed_ref, half_start(table_ref, last), places_ref, rows, wide)
    put = pltpu.make_async_copy(wide, dense_ref.at[REST - 1], sem)
    put.start()
    out_ref[...] = jnp.dot(wide[...], right_ref[last], preferred_element_type=F32) + sum_ref[...]
    put.wait()


def close(packed, table, places, right_side, total, dense):
    return pl.pallas_call(
        close_kernel,
        out_shape=(
            jax.ShapeDtypeStruct((REST, ROWS, HALF), BF16),
            jax.ShapeDtypeStruct((ROWS, 2 * W), F32),
        ),
        in_specs=[SMEM, SMEM, VMEM, VMEM, VMEM, HBM],
        out_specs=(HBM, VMEM),
        scratch_shapes=[
            pltpu.VMEM((TILES, BR + 1, B, W), F32),
            pltpu.VMEM((ROWS, HALF), BF16),
            pltpu.SemaphoreType.DMA,
        ],
        input_output_aliases={5: 0},
        compiler_params=params(50),
        cost_estimate=COST,
        name="close",
    )(table, places, packed, right_side, total, dense)


def finish_kernel(sum_ref, passed_ref, masks_ref, mine_ref, other_ref):
    scale = (NB / (KX * KX * B)) ** 0.5
    for i in range(BR):
        rows = pl.ds(i * B, B)
        for k, square_ref in enumerate((mine_ref, other_ref)):
            keep = jnp.broadcast_to(masks_ref[2 + k, i : i + 1, :], (B, W))
            value = sum_ref[rows, pl.ds(k * W, W)] + passed_ref[rows, pl.ds((1 - k) * W, W)]
            square_ref[rows, :] = jnp.where(keep > 0.0, value * scale, 0.0).astype(BF16)


def finish(total, passed, masks):
    return pl.pallas_call(
        finish_kernel,
        out_shape=(jax.ShapeDtypeStruct((ROWS, W), BF16),) * 2,
        in_specs=[VMEM] * 3,
        out_specs=(VMEM,) * 2,
        compiler_params=params(48),
        cost_estimate=COST,
        name="finish",
    )(total, passed, masks)


def cube_part(steps, table, lists, pieces, acc=None, last=None):
    scale = (NB / (KX * KSQ * B)) ** 0.5
    count = len(pieces)

    def kernel(table_ref, own_first, own_rest, other_first, other_rest, *refs):
        refs = list(refs)
        pieces_refs = [refs.pop(0) for _ in pieces]
        acc_ref = refs.pop(0) if acc is not None else None
        tile_ref, masks_ref = (refs.pop(0), refs.pop(0)) if last is not None else (None, None)
        out_ref, held, sems = refs
        y, row, core = (table_ref[4 * TILES + k] for k in range(3))
        apart = (y - row) * (1 - 2 * core)
        for h in range(2 * count):
            p, half = h // 2, h % 2
            d = jnp.bitwise_and(apart - steps[p], GROUPS - 1)
            same = core == half
            ours = jnp.logical_or(
                jnp.logical_and(same, d <= 4), jnp.logical_and(d > 0, d < 4)
            )
            d = jnp.where(d > 4, GROUPS - d, d)
            at = jnp.where(d == 0, 0, 2 * d - jnp.where(same == ours, 1, 0))
            early = at < FIRST
            held_half = held.at[p, :, pl.ds(half * HALF, HALF)]
            for mine in (True, False):
                here = ours if mine else jnp.logical_not(ours)
                begin, rest = (own_first, own_rest) if mine else (other_first, other_rest)

                @pl.when(jnp.logical_and(here, early))
                def _():
                    pltpu.make_async_copy(begin.at[at], held_half, sems.at[h]).start()

                @pl.when(jnp.logical_and(here, jnp.logical_not(early)))
                def _():
                    pltpu.make_async_copy(rest.at[at - FIRST], held_half, sems.at[h]).start()

        total = None if acc_ref is None else acc_ref[...]
        for p in range(count):
            for half in range(2):
                held_half = held.at[p, :, pl.ds(half * HALF, HALF)]
                pltpu.make_async_copy(own_first.at[0], held_half, sems.at[2 * p + half]).wait()
            term = jnp.dot(held[p], pieces_refs[p][...], preferred_element_type=F32)
            total = term if total is None else total + term
        if last is None:
            out_ref[...] = total
            return
        for k in range(BR):
            rows = pl.ds(k * B, B)
            keep_x = jnp.broadcast_to(masks_ref[0, k : k + 1, :], (B, W))
            keep_out = jnp.broadcast_to(masks_ref[1, k : k + 1, :], (B, W))
            sparse = jnp.where(keep_x > 0.0, tile_ref[rows, :].astype(F32), 0.0)
            cube = total[k * B : (k + 1) * B, :] * scale
            result = 1.5 * sparse - 0.5 * cube
            out_ref[rows, :] = jnp.where(keep_out > 0.0, result, 0.0).astype(BF16)

    operands = [table, *lists, *pieces]
    if acc is not None:
        operands.append(acc)
    if last is not None:
        operands += last
    return pl.pallas_call(
        kernel,
        out_shape=jax.ShapeDtypeStruct((ROWS, W), F32 if last is None else BF16),
        in_specs=[SMEM] + [HBM] * 4 + [VMEM] * (len(operands) - 5),
        out_specs=VMEM,
        scratch_shapes=[
            pltpu.VMEM((count, ROWS, 2 * HALF), BF16),
            pltpu.SemaphoreType.DMA((2 * count,)),
        ],
        compiler_params=params(50),
        cost_estimate=COST,
        name="cube_last" if last is not None else "cube_part",
    )(*operands)


def local(matrix, list_x, list_sq, list_out):
    layers = lax.axis_size("layer")
    col = lax.axis_index("col").astype(jnp.int32)
    row = lax.axis_index("row").astype(jnp.int32)
    layer = lax.axis_index("layer").astype(jnp.int32)
    y, core = col // 2, col % 2
    sign = 1 - 2 * core
    base = jnp.stack([(c * layers + layer) * (W // B) for c in (col, jnp.bitwise_xor(col, 1))])

    brought = [(0, 1), (1, 1), (1, 0), (2, 1), (2, 0), (3, 1), (3, 0), (4, 1)]
    table = []
    for d, same in brought:
        table += [jnp.bitwise_and(y - sign * d, GROUPS - 1), core if same else 1 - core]
    table = jnp.stack(table + [y, row, core])
    cols = 2 * GROUPS
    swap = [(c, c ^ 1) for c in range(cols)]
    turn_y = [(c, (c + (2 if c % 2 == 0 else -2)) % cols) for c in range(cols)]
    turn_z = [
        (r * cols + c, (r + (1 if c % 2 == 0 else -1)) % GROUPS * cols + c)
        for r in range(GROUPS)
        for c in range(cols)
    ]

    def along_y(piece):
        return lax.ppermute(piece, "col", turn_y)

    def along_z(piece):
        return lax.ppermute(piece, ("row", "col"), turn_z)

    def across(piece):
        return lax.ppermute(piece, "col", swap)

    def after(piece, *done):
        return lax.optimization_barrier((piece, *done))[0]

    pay, left, places = pack(base, list_x, matrix)
    pays = lax.all_gather(pay, "row", axis=0, tiled=False)
    a0 = lax.all_to_all(left, "layer", 0, 0, tiled=True)
    b0 = across(a0)
    a1, b1 = along_y(a0), along_y(b0)
    dense = widen(0, [a0], table, places)
    a2, b2 = along_y(after(a1, dense)), along_y(b1)
    dense = widen(1, [a1, b1], table, places, dense)
    a3, b3 = along_y(after(a2, dense)), along_y(b2)
    a4 = along_y(a3)
    dense = widen(3, [after(a2, a3), b2], table, places, dense)
    pays = after(pays, dense)
    right_side, masks = right(table, base, (list_x, list_sq, list_out), pays, across(pays))
    rest, total = product([a3, b3], table, places, dense, right_side)
    rest, total = close(a4, table, places, right_side, total, rest)
    c0, d0 = finish(total, across(total), masks)

    lists = (dense, rest, across(dense), across(after(rest, c0)))

    def cubed(distance, pieces, *more):
        steps = [distance] if len(pieces) == 1 else [-distance, distance]
        return cube_part(steps, table, lists, pieces, *more)

    c1, d1 = along_z(c0), along_z(d0)
    c2, d2 = along_z(c1), along_z(d1)
    c3, d3 = along_z(c2), along_z(d2)
    acc = cubed(0, [c0])
    acc = cubed(1, [c1, across(d1)], acc)
    c4 = along_z(after(c3, acc))
    acc = cubed(2, [c2, across(d2)], acc)
    acc = cubed(3, [c3, across(d3)], acc)
    return cubed(4, [c4], acc, (matrix, masks))


def solution(mesh):
    placed = (P("row", ("col", "layer")), P("row", None), P("row", None), P("row", None))
    return jax.shard_map(
        local, mesh=mesh, in_specs=placed, out_specs=P("row", ("col", "layer")), check_vma=False
    )
```

```python
import jax
import jax.numpy as jnp
from jax import lax
from jax.experimental import pallas as pl
from jax.experimental.pallas import tpu as pltpu
from jax.sharding import PartitionSpec as P

B = 32
NB = 256
KX = 40
KSQ = 60
CAP = 10
ROWS = 1024
W = 128
BR = ROWS // B
GROUPS = 8
TILES = 4
HALF = TILES * W
PAY = 576
FIRST = 2 * TILES - 1
F32 = jnp.float32
BF16 = jnp.bfloat16
MIB = 1 << 20
SMEM = pl.BlockSpec(memory_space=pltpu.SMEM)
VMEM = pl.BlockSpec(memory_space=pltpu.VMEM)
HBM = pl.BlockSpec(memory_space=pltpu.HBM)


def params(limit):
    return pltpu.CompilerParams(vmem_limit_bytes=limit * MIB)


def cost(flops, size):
    return pl.CostEstimate(flops=flops, bytes_accessed=size, transcendentals=0)


def copies_in(pairs, sems):
    copies = [pltpu.make_async_copy(a, b, sems.at[k]) for k, (a, b) in enumerate(pairs)]
    for copy in copies:
        copy.start()
    for copy in copies:
        copy.wait()


def lane_hits(lists, base):
    ids = base + lax.broadcasted_iota(jnp.int32, (BR, W), 1) // B
    hit = jnp.zeros((BR, W), F32)
    for t in range(lists.shape[1]):
        hit = jnp.where(lists[:, t : t + 1] == ids, 1.0, hit)
    return hit


def slots_of(hit):
    below = lax.broadcasted_iota(jnp.int32, (BR, BR), 1) < lax.broadcasted_iota(
        jnp.int32, (BR, BR), 0
    )
    rank = jnp.dot(
        jnp.where(below, 1.0, 0.0).astype(BF16), hit.astype(BF16), preferred_element_type=F32
    )
    return jnp.where(hit > 0.0, rank, float(CAP))


def pack_kernel(base_ref, list_hbm, tile_hbm, pay_ref, left_ref, places_ref, list_ref, tile_ref, sems):
    copies_in([(list_hbm, list_ref), (tile_hbm, tile_ref)], sems)
    lists = list_ref[...]
    hit = lane_hits(lists, base_ref[0])
    slot = slots_of(hit)
    slot_int = slot.astype(jnp.int32)
    packed = [jnp.zeros((B, W), F32) for _ in range(CAP)]
    for i in range(BR):
        block = tile_ref[pl.ds(i * B, B), :].astype(F32)
        row = jnp.broadcast_to(slot_int[i : i + 1, :], (B, W))
        for s in range(min(i + 1, CAP)):
            packed[s] = jnp.where(row == s, block, packed[s])
    for s in range(CAP):
        value = packed[s].astype(BF16)
        pay_ref[pl.ds(s * B, B), :] = value
        for x in range(TILES):
            left_ref[x, s] = value
    pay_ref[pl.ds(CAP * B, B), :] = slot.astype(BF16)
    pay_ref[pl.ds((CAP + 1) * B, PAY - (CAP + 1) * B), :] = jnp.zeros(
        (PAY - (CAP + 1) * B, W), BF16
    )

    ids = lax.broadcasted_iota(jnp.int32, (BR, NB), 1)
    every = jnp.zeros((BR, NB), F32)
    for t in range(KX):
        every = jnp.where(lists[:, t : t + 1] == ids, 1.0, every)
    slot = slots_of(every)
    rows = lax.broadcasted_iota(jnp.int32, (BR, NB), 0).astype(F32) - BR
    for s in range(CAP):
        at = jnp.sum(jnp.where(slot == s, rows, 0.0), axis=0, keepdims=True) + BR
        places_ref[pl.ds(s, 1), :] = at.astype(jnp.int32)


def pack(base, list_x, tile):
    return pl.pallas_call(
        pack_kernel,
        out_shape=(
            jax.ShapeDtypeStruct((PAY, W), BF16),
            jax.ShapeDtypeStruct((TILES, CAP, B, W), BF16),
            jax.ShapeDtypeStruct((CAP, NB), jnp.int32),
        ),
        in_specs=[SMEM, HBM, HBM],
        out_specs=(VMEM,) * 3,
        scratch_shapes=[
            pltpu.VMEM((BR, KX), jnp.int32),
            pltpu.VMEM((ROWS, W), BF16),
            pltpu.SemaphoreType.DMA((2,)),
        ],
        compiler_params=params(48),
        cost_estimate=cost(10_000_000, 500_000),
        name="pack",
    )(base, list_x, tile)


def right_kernel(table_ref, base_ref, *refs):
    lists_hbm, mine_hbm, other_hbm, right_ref, masks_ref = refs[:3], *refs[3:7]
    lists, pays_ref, sems = refs[7:10], refs[10], refs[11]
    rows = pl.ds(0, (CAP + 1) * B)
    pairs = list(zip(lists_hbm, lists))
    pairs += [(ref.at[:, rows], pays_ref.at[k]) for k, ref in enumerate((mine_hbm, other_hbm))]
    copies_in(pairs, sems)
    for k in range(3):
        masks_ref[k] = lane_hits(lists[k][...], base_ref[0])

    @pl.loop(0, 2 * TILES)
    def _(h):
        g, core = table_ref[2 * h], table_ref[2 * h + 1]
        first = pl.multiple_of(CAP * B + core * (BR // 2), BR // 2)
        for k in range(2):
            part = [pays_ref[k, g, pl.ds(s * B, B), :].astype(F32) for s in range(CAP)]
            slot = pays_ref[k, g, pl.ds(first, BR // 2), :].astype(F32).astype(jnp.int32)
            for t in range(BR // 2):
                row = jnp.broadcast_to(slot[t : t + 1, :], (B, W))
                value = jnp.zeros((B, W), F32)
                for s in range(CAP):
                    value = jnp.where(row == s, part[s], value)
                right_ref[h, pl.ds(t * B, B), pl.ds(k * W, W)] = value.astype(BF16)


def right(table, base, lists, mine, other):
    return pl.pallas_call(
        right_kernel,
        out_shape=(
            jax.ShapeDtypeStruct((2 * TILES, HALF, 2 * W), BF16),
            jax.ShapeDtypeStruct((3, BR, W), F32),
        ),
        in_specs=[SMEM, SMEM] + [HBM] * 5,
        out_specs=(VMEM, VMEM),
        scratch_shapes=[pltpu.VMEM(a.shape, jnp.int32) for a in lists]
        + [
            pltpu.VMEM((2, GROUPS, (CAP + 1) * B, W), BF16),
            pltpu.SemaphoreType.DMA((5,)),
        ],
        compiler_params=params(48),
        cost_estimate=cost(40_000_000, 4 * MIB),
        name="right",
    )(table, base, *lists, mine, other)


def unpack(packed_ref, start, places_ref, rows, wide):
    lane = lax.broadcasted_iota(jnp.int32, (B, W), 1) // B
    masks = [lane == c for c in range(W // B)]
    for q in range(TILES):
        rows[q, pl.ds(0, BR)] = jnp.zeros((BR, B, W), F32)
    for q in range(TILES):
        for s in range(CAP):
            block = packed_ref[q, s].astype(F32)
            for c in range(W // B):
                row = places_ref[s, start + q * (W // B) + c]
                pltpu.store(rows.at[q, row], block, mask=masks[c])
    for q in range(TILES):
        for i in range(BR):
            wide[pl.ds(i * B, B), pl.ds(q * W, W)] = rows[q, i].astype(BF16)


def half_start(table_ref, k):
    return (table_ref[2 * k] * 2 + table_ref[2 * k + 1]) * (HALF // B)


def widen(first, halves, table, places):
    count = len(halves)

    def kernel(table_ref, places_ref, *refs):
        dense_ref, rows = refs[count:]
        for k in range(count):
            unpack(refs[k], half_start(table_ref, first + k), places_ref, rows, dense_ref.at[k])

    return pl.pallas_call(
        kernel,
        out_shape=jax.ShapeDtypeStruct((count, ROWS, HALF), BF16),
        in_specs=[SMEM, SMEM] + [VMEM] * count,
        out_specs=VMEM,
        scratch_shapes=[pltpu.VMEM((TILES, BR + 1, B, W), F32)],
        compiler_params=params(24),
        cost_estimate=cost(4 * ROWS * HALF * W * count, count * 3 * MIB),
        name="widen",
    )(table, places, *halves)


def product(halves, table, places, lists, right_side):
    count = len(halves)
    sizes = [array.shape[0] for array in lists] + [count]
    first = sum(sizes) - count

    def kernel(table_ref, places_ref, *refs):
        packed, refs = refs[:count], refs[count:]
        right_ref, parts, sum_ref, rows = refs[0], refs[1:-2], refs[-2], refs[-1]
        for k in range(count):
            unpack(packed[k], half_start(table_ref, first + k), places_ref, rows, parts[-1].at[k])

        @pl.loop(0, ROWS // STEP)
        def _(i):
            part = pl.ds(pl.multiple_of(i * STEP, STEP), STEP)
            at, total = 0, None
            for ref, size in zip(parts, sizes):
                for k in range(size):
                    term = jnp.dot(ref[k, part, :], right_ref[at], preferred_element_type=F32)
                    at, total = at + 1, term if total is None else total + term
            sum_ref[part, :] = total

    return pl.pallas_call(
        kernel,
        out_shape=(
            jax.ShapeDtypeStruct((count, ROWS, HALF), BF16),
            jax.ShapeDtypeStruct((ROWS, 2 * W), F32),
        ),
        in_specs=[SMEM, SMEM] + [VMEM] * (count + 1 + len(lists)),
        out_specs=(VMEM, VMEM),
        scratch_shapes=[pltpu.VMEM((TILES, BR + 1, B, W), F32)],
        compiler_params=params(24),
        cost_estimate=cost(16 * ROWS * HALF * W, 12 * MIB),
        name="product",
    )(table, places, *halves, right_side, *lists)


STEP = 256


def close_kernel(
    table_ref, places_ref, packed_ref, right_ref, sum_ref, dense_ref, mine_ref, other_ref, rows
):
    unpack(packed_ref, half_start(table_ref, FIRST), places_ref, rows, dense_ref.at[0])
    total = jnp.dot(dense_ref[0], right_ref[FIRST], preferred_element_type=F32) + sum_ref[...]
    mine_ref[...] = total[:, :W]
    other_ref[...] = total[:, W:]


def close(packed, table, places, right_side, total):
    return pl.pallas_call(
        close_kernel,
        out_shape=(jax.ShapeDtypeStruct((1, ROWS, HALF), BF16),)
        + (jax.ShapeDtypeStruct((ROWS, W), F32),) * 2,
        in_specs=[SMEM, SMEM, VMEM, VMEM, VMEM],
        out_specs=(VMEM,) * 3,
        scratch_shapes=[pltpu.VMEM((TILES, BR + 1, B, W), F32)],
        compiler_params=params(32),
        cost_estimate=cost(4 * ROWS * HALF * W, 3 * MIB),
        name="close",
    )(table, places, packed, right_side, total)


def finish_kernel(mine_ref, other_ref, masks_ref, square_ref):
    scale = (NB / (KX * KX * B)) ** 0.5
    for i in range(BR):
        rows = pl.ds(i * B, B)
        keep = jnp.broadcast_to(masks_ref[1, i : i + 1, :], (B, W))
        value = (mine_ref[rows, :] + other_ref[rows, :]) * scale
        square_ref[rows, :] = jnp.where(keep > 0.0, value, 0.0).astype(BF16)


def finish(mine, other, masks):
    return pl.pallas_call(
        finish_kernel,
        out_shape=jax.ShapeDtypeStruct((ROWS, W), BF16),
        in_specs=[VMEM] * 3,
        out_specs=VMEM,
        compiler_params=params(32),
        cost_estimate=cost(400_000, MIB),
        name="finish",
    )(mine, other, masks)


def cube_kernel(table_ref, *refs):
    *lists, square_ref, tile_ref, masks_ref, out_ref, acc = refs
    scale = (NB / (KX * KSQ * B)) ** 0.5
    at = 0
    for ref in lists:
        for k in range(ref.shape[0]):
            g, core = table_ref[at], table_ref[at + 1]
            half = square_ref[g, pl.ds(pl.multiple_of(core * HALF, HALF), HALF), :]
            term = jnp.dot(ref[k], half, preferred_element_type=F32)
            acc[...] = term if at == 0 else acc[...] + term
            at += 2
    for k in range(BR):
        rows = pl.ds(k * B, B)
        keep_x = jnp.broadcast_to(masks_ref[0, k : k + 1, :], (B, W))
        keep_out = jnp.broadcast_to(masks_ref[2, k : k + 1, :], (B, W))
        sparse = jnp.where(keep_x > 0.0, tile_ref[rows, :].astype(F32), 0.0)
        result = 1.5 * sparse - 0.5 * (acc[rows, :] * scale)
        out_ref[rows, :] = jnp.where(keep_out > 0.0, result, 0.0).astype(BF16)


def cube(table, lists, squares, tile, masks):
    return pl.pallas_call(
        cube_kernel,
        out_shape=jax.ShapeDtypeStruct((ROWS, W), BF16),
        in_specs=[SMEM] + [VMEM] * (len(lists) + 3),
        out_specs=VMEM,
        scratch_shapes=[pltpu.VMEM((ROWS, W), F32)],
        compiler_params=params(24),
        cost_estimate=cost(2 * GROUPS * ROWS * ROWS * W, 20 * MIB),
        name="cube",
    )(table, *lists, squares, tile, masks)


def local(matrix, list_x, list_sq, list_out):
    layers = lax.axis_size("layer")
    col = lax.axis_index("col").astype(jnp.int32)
    layer = lax.axis_index("layer").astype(jnp.int32)
    y, core = col // 2, col % 2
    sign = 1 - 2 * core
    base = jnp.reshape((col * layers + layer) * (W // B), (1,))

    brought = [(0, 1), (1, 1), (1, 0), (2, 1), (2, 0), (3, 1), (3, 0), (4, 1)]
    table = []
    for turn, own in ((-sign, core), (sign, 1 - core)):
        for d, same in brought:
            table += [jnp.bitwise_and(y + turn * d, GROUPS - 1), own if same else 1 - own]
    table = jnp.stack(table)

    cols = 2 * GROUPS
    swap = [(c, c ^ 1) for c in range(cols)]
    turn_y = [(c, (c + (2 if c % 2 == 0 else -2)) % cols) for c in range(cols)]

    def along_y(piece):
        return lax.ppermute(piece, "col", turn_y)

    def across(piece):
        return lax.ppermute(piece, "col", swap)

    def after(piece, *done):
        return lax.optimization_barrier((piece, *done))[0]

    pay, left, places = pack(base, list_x, matrix)
    pays = lax.all_gather(pay, "row", axis=0, tiled=False)
    a0 = lax.all_to_all(left, "layer", 0, 0, tiled=True)
    b0 = across(a0)
    a1, b1 = along_y(a0), along_y(b0)
    lists = [widen(0, [a0], table, places)]
    a2, b2 = along_y(after(a1, lists[-1])), along_y(b1)
    lists.append(widen(1, [a1, b1], table, places))
    a3, b3 = along_y(after(a2, lists[-1])), along_y(b2)
    lists.append(widen(3, [a2, b2], table, places))
    a4 = along_y(after(a3, lists[-1]))
    pays = after(pays, lists[-1], a3, b3)
    right_side, masks = right(table, base, (list_x, list_sq, list_out), pays, across(pays))
    dense, total = product([a3, b3], table, places, lists, right_side)
    end, mine, other = close(a4, table, places, right_side, total)
    square = finish(mine, across(other), masks)

    squares = lax.all_gather(square, "row", axis=0, tiled=False)
    lists += [dense, end]
    lists += [across(part) for part in lists]
    return cube(table, lists, squares, matrix, masks)


def solution(mesh):
    placed = (P("row", ("col", "layer")), P("row", None), P("row", None), P("row", None))
    return jax.shard_map(
        local, mesh=mesh, in_specs=placed, out_specs=P("row", ("col", "layer")), check_vma=False
    )
```

```python
import jax
import jax.numpy as jnp
from jax import lax
from jax.experimental import pallas as pl
from jax.experimental.pallas import tpu as pltpu
from jax.sharding import PartitionSpec as P

B = 32
NB = 256
KX = 40
KSQ = 60
CAP = 10
ROWS = 1024
W = 128
BR = ROWS // B
GROUPS = 8
TILES = 4
HALF = TILES * W
PAY = 576
FIRST = 2 * TILES - 1
F32 = jnp.float32
BF16 = jnp.bfloat16
MIB = 1 << 20
SMEM = pl.BlockSpec(memory_space=pltpu.SMEM)
VMEM = pl.BlockSpec(memory_space=pltpu.VMEM)
HBM = pl.BlockSpec(memory_space=pltpu.HBM)


def params(limit):
    return pltpu.CompilerParams(vmem_limit_bytes=limit * MIB)


def cost(flops, size):
    return pl.CostEstimate(flops=flops, bytes_accessed=size, transcendentals=0)


def copies_in(pairs, sems):
    copies = [pltpu.make_async_copy(a, b, sems.at[k]) for k, (a, b) in enumerate(pairs)]
    for copy in copies:
        copy.start()
    for copy in copies:
        copy.wait()


def lane_hits(lists, base):
    ids = base + lax.broadcasted_iota(jnp.int32, (BR, W), 1) // B
    hit = jnp.zeros((BR, W), F32)
    for t in range(lists.shape[1]):
        hit = jnp.where(lists[:, t : t + 1] == ids, 1.0, hit)
    return hit


def slots_of(hit):
    below = lax.broadcasted_iota(jnp.int32, (BR, BR), 1) < lax.broadcasted_iota(
        jnp.int32, (BR, BR), 0
    )
    rank = jnp.dot(
        jnp.where(below, 1.0, 0.0).astype(BF16), hit.astype(BF16), preferred_element_type=F32
    )
    return jnp.where(hit > 0.0, rank, float(CAP))


def pack_kernel(base_ref, list_hbm, tile_hbm, pay_ref, left_ref, places_ref, list_ref, tile_ref, sems):
    copies_in([(list_hbm, list_ref), (tile_hbm, tile_ref)], sems)
    lists = list_ref[...]
    hit = lane_hits(lists, base_ref[0])
    slot = slots_of(hit)
    slot_int = slot.astype(jnp.int32)
    packed = [jnp.zeros((B, W), F32) for _ in range(CAP)]
    for i in range(BR):
        block = tile_ref[pl.ds(i * B, B), :].astype(F32)
        row = jnp.broadcast_to(slot_int[i : i + 1, :], (B, W))
        for s in range(min(i + 1, CAP)):
            packed[s] = jnp.where(row == s, block, packed[s])
    for s in range(CAP):
        value = packed[s].astype(BF16)
        pay_ref[pl.ds(s * B, B), :] = value
        for x in range(TILES):
            left_ref[x, s] = value
    pay_ref[pl.ds(CAP * B, B), :] = slot.astype(BF16)
    pay_ref[pl.ds((CAP + 1) * B, PAY - (CAP + 1) * B), :] = jnp.zeros(
        (PAY - (CAP + 1) * B, W), BF16
    )

    ids = lax.broadcasted_iota(jnp.int32, (BR, NB), 1)
    every = jnp.zeros((BR, NB), F32)
    for t in range(KX):
        every = jnp.where(lists[:, t : t + 1] == ids, 1.0, every)
    slot = slots_of(every)
    rows = lax.broadcasted_iota(jnp.int32, (BR, NB), 0).astype(F32) - BR
    for s in range(CAP):
        at = jnp.sum(jnp.where(slot == s, rows, 0.0), axis=0, keepdims=True) + BR
        places_ref[pl.ds(s, 1), :] = at.astype(jnp.int32)


def pack(base, list_x, tile):
    return pl.pallas_call(
        pack_kernel,
        out_shape=(
            jax.ShapeDtypeStruct((PAY, W), BF16),
            jax.ShapeDtypeStruct((TILES, CAP, B, W), BF16),
            jax.ShapeDtypeStruct((CAP, NB), jnp.int32),
        ),
        in_specs=[SMEM, HBM, HBM],
        out_specs=(VMEM,) * 3,
        scratch_shapes=[
            pltpu.VMEM((BR, KX), jnp.int32),
            pltpu.VMEM((ROWS, W), BF16),
            pltpu.SemaphoreType.DMA((2,)),
        ],
        compiler_params=params(6),
        cost_estimate=cost(10_000_000, 500_000),
        name="pack",
    )(base, list_x, tile)


def masks_kernel(base_ref, x_ref, sq_ref, out_ref, masks_ref):
    for k, lists in enumerate((x_ref, sq_ref, out_ref)):
        masks_ref[k] = lane_hits(lists[...], base_ref[0])


def masks_of(base, lists):
    return pl.pallas_call(
        masks_kernel,
        out_shape=jax.ShapeDtypeStruct((3, BR, W), F32),
        in_specs=[SMEM] + [VMEM] * 3,
        out_specs=VMEM,
        compiler_params=params(4),
        cost_estimate=cost(1_000_000, 100_000),
        name="masks",
    )(base, *lists)


def right_kernel(table_ref, mine_hbm, other_hbm, right_ref, pays_ref, sems):
    rows = pl.ds(0, (CAP + 1) * B)
    pairs = [(ref.at[:, rows], pays_ref.at[k]) for k, ref in enumerate((mine_hbm, other_hbm))]
    copies_in(pairs, sems)

    @pl.loop(0, 2 * TILES)
    def _(h):
        g, core = table_ref[2 * h], table_ref[2 * h + 1]
        first = pl.multiple_of(CAP * B + core * (BR // 2), BR // 2)
        for k in range(2):
            part = [pays_ref[k, g, pl.ds(s * B, B), :].astype(F32) for s in range(CAP)]
            slot = pays_ref[k, g, pl.ds(first, BR // 2), :].astype(F32).astype(jnp.int32)
            for t in range(BR // 2):
                row = jnp.broadcast_to(slot[t : t + 1, :], (B, W))
                value = jnp.zeros((B, W), F32)
                for s in range(CAP):
                    value = jnp.where(row == s, part[s], value)
                right_ref[h, pl.ds(t * B, B), pl.ds(k * W, W)] = value.astype(BF16)


def right(table, mine, other):
    return pl.pallas_call(
        right_kernel,
        out_shape=jax.ShapeDtypeStruct((2 * TILES, HALF, 2 * W), BF16),
        in_specs=[SMEM] + [HBM] * 2,
        out_specs=VMEM,
        scratch_shapes=[
            pltpu.VMEM((2, GROUPS, (CAP + 1) * B, W), BF16),
            pltpu.SemaphoreType.DMA((2,)),
        ],
        compiler_params=params(12),
        cost_estimate=cost(40_000_000, 4 * MIB),
        name="right",
    )(table, mine, other)


def unpack(packed_ref, start, places_ref, rows, wide):
    lane = lax.broadcasted_iota(jnp.int32, (B, W), 1) // B
    masks = [lane == c for c in range(W // B)]
    for q in range(TILES):
        rows[q, pl.ds(0, BR)] = jnp.zeros((BR, B, W), F32)
    for q in range(TILES):
        for s in range(CAP):
            block = packed_ref[q, s].astype(F32)
            for c in range(W // B):
                row = places_ref[s, start + q * (W // B) + c]
                pltpu.store(rows.at[q, row], block, mask=masks[c])
    for q in range(TILES):
        for i in range(BR):
            wide[pl.ds(i * B, B), pl.ds(q * W, W)] = rows[q, i].astype(BF16)


def half_start(table_ref, k):
    return (table_ref[2 * k] * 2 + table_ref[2 * k + 1]) * (HALF // B)


def widen(first, halves, table, places):
    count = len(halves)

    def kernel(table_ref, places_ref, *refs):
        dense_ref, rows = refs[count:]
        for k in range(count):
            unpack(refs[k], half_start(table_ref, first + k), places_ref, rows, dense_ref.at[k])

    return pl.pallas_call(
        kernel,
        out_shape=jax.ShapeDtypeStruct((count, ROWS, HALF), BF16),
        in_specs=[SMEM, SMEM] + [VMEM] * count,
        out_specs=VMEM,
        scratch_shapes=[pltpu.VMEM((TILES, BR + 1, B, W), F32)],
        compiler_params=params(6),
        cost_estimate=cost(4 * ROWS * HALF * W * count, count * 3 * MIB),
        name="widen",
    )(table, places, *halves)


def product(halves, table, places, lists, right_side):
    count = len(halves)
    sizes = [array.shape[0] for array in lists] + [count]
    first = sum(sizes) - count

    def kernel(table_ref, places_ref, *refs):
        packed, refs = refs[:count], refs[count:]
        right_ref, parts, sum_ref, rows = refs[0], refs[1:-2], refs[-2], refs[-1]
        for k in range(count):
            unpack(packed[k], half_start(table_ref, first + k), places_ref, rows, parts[-1].at[k])

        @pl.loop(0, ROWS // STEP)
        def _(i):
            part = pl.ds(pl.multiple_of(i * STEP, STEP), STEP)
            at, total = 0, None
            for ref, size in zip(parts, sizes):
                for k in range(size):
                    term = jnp.dot(ref[k, part, :], right_ref[at], preferred_element_type=F32)
                    at, total = at + 1, term if total is None else total + term
            sum_ref[part, :] = total

    return pl.pallas_call(
        kernel,
        out_shape=(
            jax.ShapeDtypeStruct((count, ROWS, HALF), BF16),
            jax.ShapeDtypeStruct((ROWS, 2 * W), F32),
        ),
        in_specs=[SMEM, SMEM] + [VMEM] * (count + 1 + len(lists)),
        out_specs=(VMEM, VMEM),
        scratch_shapes=[pltpu.VMEM((TILES, BR + 1, B, W), F32)],
        compiler_params=params(8),
        cost_estimate=cost(16 * ROWS * HALF * W, 12 * MIB),
        name="product",
    )(table, places, *halves, right_side, *lists)


STEP = 256


def close_kernel(
    table_ref, places_ref, packed_ref, right_ref, sum_ref, dense_ref, mine_ref, other_ref, rows
):
    unpack(packed_ref, half_start(table_ref, FIRST), places_ref, rows, dense_ref.at[0])
    total = jnp.dot(dense_ref[0], right_ref[FIRST], preferred_element_type=F32) + sum_ref[...]
    mine_ref[...] = total[:, :W]
    other_ref[...] = total[:, W:]


def close(packed, table, places, right_side, total):
    return pl.pallas_call(
        close_kernel,
        out_shape=(jax.ShapeDtypeStruct((1, ROWS, HALF), BF16),)
        + (jax.ShapeDtypeStruct((ROWS, W), F32),) * 2,
        in_specs=[SMEM, SMEM, VMEM, VMEM, VMEM],
        out_specs=(VMEM,) * 3,
        scratch_shapes=[pltpu.VMEM((TILES, BR + 1, B, W), F32)],
        compiler_params=params(8),
        cost_estimate=cost(4 * ROWS * HALF * W, 3 * MIB),
        name="close",
    )(table, places, packed, right_side, total)


def finish_kernel(mine_ref, other_ref, masks_ref, square_ref):
    scale = (NB / (KX * KX * B)) ** 0.5
    for i in range(BR):
        rows = pl.ds(i * B, B)
        keep = jnp.broadcast_to(masks_ref[1, i : i + 1, :], (B, W))
        value = (mine_ref[rows, :] + other_ref[rows, :]) * scale
        square_ref[rows, :] = jnp.where(keep > 0.0, value, 0.0).astype(BF16)


def finish(mine, other, masks):
    return pl.pallas_call(
        finish_kernel,
        out_shape=jax.ShapeDtypeStruct((ROWS, W), BF16),
        in_specs=[VMEM] * 3,
        out_specs=VMEM,
        compiler_params=params(4),
        cost_estimate=cost(400_000, MIB),
        name="finish",
    )(mine, other, masks)


def cube_kernel(table_ref, *refs):
    *lists, square_ref, tile_ref, masks_ref, out_ref, acc = refs
    scale = (NB / (KX * KSQ * B)) ** 0.5
    at = 0
    for ref in lists:
        for k in range(ref.shape[0]):
            g, core = table_ref[at], table_ref[at + 1]
            half = square_ref[g, pl.ds(pl.multiple_of(core * HALF, HALF), HALF), :]
            term = jnp.dot(ref[k], half, preferred_element_type=F32)
            acc[...] = term if at == 0 else acc[...] + term
            at += 2
    for k in range(BR):
        rows = pl.ds(k * B, B)
        keep_x = jnp.broadcast_to(masks_ref[0, k : k + 1, :], (B, W))
        keep_out = jnp.broadcast_to(masks_ref[2, k : k + 1, :], (B, W))
        sparse = jnp.where(keep_x > 0.0, tile_ref[rows, :].astype(F32), 0.0)
        result = 1.5 * sparse - 0.5 * (acc[rows, :] * scale)
        out_ref[rows, :] = jnp.where(keep_out > 0.0, result, 0.0).astype(BF16)


def cube(table, lists, squares, tile, masks):
    return pl.pallas_call(
        cube_kernel,
        out_shape=jax.ShapeDtypeStruct((ROWS, W), BF16),
        in_specs=[SMEM] + [VMEM] * (len(lists) + 3),
        out_specs=VMEM,
        scratch_shapes=[pltpu.VMEM((ROWS, W), F32)],
        compiler_params=params(8),
        cost_estimate=cost(2 * GROUPS * ROWS * ROWS * W, 20 * MIB),
        name="cube",
    )(table, *lists, squares, tile, masks)


def local(matrix, list_x, list_sq, list_out):
    layers = lax.axis_size("layer")
    col = lax.axis_index("col").astype(jnp.int32)
    layer = lax.axis_index("layer").astype(jnp.int32)
    y, core = col // 2, col % 2
    sign = 1 - 2 * core
    base = jnp.reshape((col * layers + layer) * (W // B), (1,))

    brought = [(0, 1), (1, 1), (1, 0), (2, 1), (2, 0), (3, 1), (3, 0), (4, 1)]
    table = []
    for turn, own in ((-sign, core), (sign, 1 - core)):
        for d, same in brought:
            table += [jnp.bitwise_and(y + turn * d, GROUPS - 1), own if same else 1 - own]
    table = jnp.stack(table)

    cols = 2 * GROUPS
    swap = [(c, c ^ 1) for c in range(cols)]
    turn_y = [(c, (c + (2 if c % 2 == 0 else -2)) % cols) for c in range(cols)]

    def along_y(piece):
        return lax.ppermute(piece, "col", turn_y)

    def across(piece):
        return lax.ppermute(piece, "col", swap)

    def after(piece, *done):
        return lax.optimization_barrier((piece, *done))[0]

    pay, left, places = pack(base, list_x, matrix)
    pays = lax.all_gather(pay, "row", axis=0, tiled=False)
    a0 = lax.all_to_all(left, "layer", 0, 0, tiled=True)
    b0 = across(a0)
    a1, b1 = along_y(a0), along_y(b0)
    masks = masks_of(base, (list_x, list_sq, list_out))
    lists = [widen(0, [after(a0, masks)], table, places)]
    a2, b2 = along_y(after(a1, lists[-1])), along_y(b1)
    lists.append(widen(1, [a1, b1], table, places))
    a3, b3 = along_y(after(a2, lists[-1])), along_y(b2)
    lists.append(widen(3, [a2, b2], table, places))
    a4 = along_y(after(a3, lists[-1]))
    pays = after(pays, lists[-1], a3, b3)
    right_side = right(table, pays, across(pays))
    dense, total = product([a3, b3], table, places, lists, right_side)
    end, mine, other = close(a4, table, places, right_side, total)
    square = finish(mine, across(other), masks)

    squares = lax.all_gather(square, "row", axis=0, tiled=False)
    lists += [dense, end]
    lists += [across(part) for part in lists]
    return cube(table, lists, squares, matrix, masks)


def solution(mesh):
    placed = (P("row", ("col", "layer")), P("row", None), P("row", None), P("row", None))
    return jax.shard_map(
        local, mesh=mesh, in_specs=placed, out_specs=P("row", ("col", "layer")), check_vma=False
    )
```

```python
import jax
import jax.numpy as jnp
from jax import lax
from jax.experimental import pallas as pl
from jax.experimental.pallas import tpu as pltpu
from jax.sharding import PartitionSpec as P

B = 32
NB = 256
KX = 40
KSQ = 60
CAP = 10
ROWS = 1024
W = 128
BR = ROWS // B
GROUPS = 8
TILES = 4
HALF = TILES * W
PAY = 576
FIRST = 2 * TILES - 1
F32 = jnp.float32
BF16 = jnp.bfloat16
MIB = 1 << 20
SMEM = pl.BlockSpec(memory_space=pltpu.SMEM)
VMEM = pl.BlockSpec(memory_space=pltpu.VMEM)
HBM = pl.BlockSpec(memory_space=pltpu.HBM)


def params(limit):
    return pltpu.CompilerParams(vmem_limit_bytes=limit * MIB)


def cost(flops, size):
    return pl.CostEstimate(flops=flops, bytes_accessed=size, transcendentals=0)


def copies_in(pairs, sems):
    copies = [pltpu.make_async_copy(a, b, sems.at[k]) for k, (a, b) in enumerate(pairs)]
    for copy in copies:
        copy.start()
    for copy in copies:
        copy.wait()


def lane_hits(lists, base):
    ids = base + lax.broadcasted_iota(jnp.int32, (BR, W), 1) // B
    hit = jnp.zeros((BR, W), F32)
    for t in range(lists.shape[1]):
        hit = jnp.where(lists[:, t : t + 1] == ids, 1.0, hit)
    return hit


def slots_of(hit):
    below = lax.broadcasted_iota(jnp.int32, (BR, BR), 1) < lax.broadcasted_iota(
        jnp.int32, (BR, BR), 0
    )
    rank = jnp.dot(
        jnp.where(below, 1.0, 0.0).astype(BF16), hit.astype(BF16), preferred_element_type=F32
    )
    return jnp.where(hit > 0.0, rank, float(CAP))


def pack_kernel(base_ref, list_hbm, tile_hbm, pay_ref, left_ref, places_ref, list_ref, tile_ref, sems):
    copies_in([(list_hbm, list_ref), (tile_hbm, tile_ref)], sems)
    lists = list_ref[...]
    hit = lane_hits(lists, base_ref[0])
    slot = slots_of(hit)
    slot_int = slot.astype(jnp.int32)
    packed = [jnp.zeros((B, W), F32) for _ in range(CAP)]
    for i in range(BR):
        block = tile_ref[pl.ds(i * B, B), :].astype(F32)
        row = jnp.broadcast_to(slot_int[i : i + 1, :], (B, W))
        for s in range(min(i + 1, CAP)):
            packed[s] = jnp.where(row == s, block, packed[s])
    for s in range(CAP):
        value = packed[s].astype(BF16)
        pay_ref[pl.ds(s * B, B), :] = value
        for x in range(TILES):
            left_ref[x, s] = value
    pay_ref[pl.ds(CAP * B, B), :] = slot.astype(BF16)
    pay_ref[pl.ds((CAP + 1) * B, PAY - (CAP + 1) * B), :] = jnp.zeros(
        (PAY - (CAP + 1) * B, W), BF16
    )

    ids = lax.broadcasted_iota(jnp.int32, (BR, NB), 1)
    every = jnp.zeros((BR, NB), F32)
    for t in range(KX):
        every = jnp.where(lists[:, t : t + 1] == ids, 1.0, every)
    slot = slots_of(every)
    rows = lax.broadcasted_iota(jnp.int32, (BR, NB), 0).astype(F32) - BR
    for s in range(CAP):
        at = jnp.sum(jnp.where(slot == s, rows, 0.0), axis=0, keepdims=True) + BR
        places_ref[pl.ds(s, 1), :] = at.astype(jnp.int32)


def pack(base, list_x, tile):
    return pl.pallas_call(
        pack_kernel,
        out_shape=(
            jax.ShapeDtypeStruct((PAY, W), BF16),
            jax.ShapeDtypeStruct((TILES, CAP, B, W), BF16),
            jax.ShapeDtypeStruct((CAP, NB), jnp.int32),
        ),
        in_specs=[SMEM, HBM, HBM],
        out_specs=(VMEM,) * 3,
        scratch_shapes=[
            pltpu.VMEM((BR, KX), jnp.int32),
            pltpu.VMEM((ROWS, W), BF16),
            pltpu.SemaphoreType.DMA((2,)),
        ],
        compiler_params=params(6),
        cost_estimate=cost(10_000_000, 500_000),
        name="pack",
    )(base, list_x, tile)


def masks_kernel(base_ref, x_ref, sq_ref, out_ref, masks_ref):
    for k, lists in enumerate((x_ref, sq_ref, out_ref)):
        masks_ref[k] = lane_hits(lists[...], base_ref[0])


def masks_of(base, lists):
    return pl.pallas_call(
        masks_kernel,
        out_shape=jax.ShapeDtypeStruct((3, BR, W), F32),
        in_specs=[SMEM] + [VMEM] * 3,
        out_specs=VMEM,
        compiler_params=params(4),
        cost_estimate=cost(1_000_000, 100_000),
        name="masks",
    )(base, *lists)


def right_kernel(table_ref, mine_hbm, other_hbm, right_ref, pays_ref, sems):
    rows = pl.ds(0, (CAP + 1) * B)
    pairs = [(ref.at[:, rows], pays_ref.at[k]) for k, ref in enumerate((mine_hbm, other_hbm))]
    copies_in(pairs, sems)

    @pl.loop(0, 2 * TILES)
    def _(h):
        g, core = table_ref[2 * h], table_ref[2 * h + 1]
        first = pl.multiple_of(CAP * B + core * (BR // 2), BR // 2)
        for k in range(2):
            part = [pays_ref[k, g, pl.ds(s * B, B), :].astype(F32) for s in range(CAP)]
            slot = pays_ref[k, g, pl.ds(first, BR // 2), :].astype(F32).astype(jnp.int32)
            for t in range(BR // 2):
                row = jnp.broadcast_to(slot[t : t + 1, :], (B, W))
                value = jnp.zeros((B, W), F32)
                for s in range(CAP):
                    value = jnp.where(row == s, part[s], value)
                right_ref[h, pl.ds(t * B, B), pl.ds(k * W, W)] = value.astype(BF16)


def right(table, mine, other):
    return pl.pallas_call(
        right_kernel,
        out_shape=jax.ShapeDtypeStruct((2 * TILES, HALF, 2 * W), BF16),
        in_specs=[SMEM] + [HBM] * 2,
        out_specs=VMEM,
        scratch_shapes=[
            pltpu.VMEM((2, GROUPS, (CAP + 1) * B, W), BF16),
            pltpu.SemaphoreType.DMA((2,)),
        ],
        compiler_params=params(12),
        cost_estimate=cost(40_000_000, 4 * MIB),
        name="right",
    )(table, mine, other)


def unpack(packed_ref, start, places_ref, rows, wide):
    lane = lax.broadcasted_iota(jnp.int32, (B, W), 1) // B
    masks = [lane == c for c in range(W // B)]
    for q in range(TILES):
        rows[q, pl.ds(0, BR)] = jnp.zeros((BR, B, W), F32)
    for q in range(TILES):
        for s in range(CAP):
            block = packed_ref[q, s].astype(F32)
            for c in range(W // B):
                row = places_ref[s, start + q * (W // B) + c]
                pltpu.store(rows.at[q, row], block, mask=masks[c])
    for q in range(TILES):
        for i in range(BR):
            wide[pl.ds(i * B, B), pl.ds(q * W, W)] = rows[q, i].astype(BF16)


def half_start(table_ref, k):
    return (table_ref[2 * k] * 2 + table_ref[2 * k + 1]) * (HALF // B)


def widen(first, halves, table, places):
    count = len(halves)

    def kernel(table_ref, places_ref, *refs):
        dense_ref, rows = refs[count:]
        for k in range(count):
            unpack(refs[k], half_start(table_ref, first + k), places_ref, rows, dense_ref.at[k])

    return pl.pallas_call(
        kernel,
        out_shape=jax.ShapeDtypeStruct((count, ROWS, HALF), BF16),
        in_specs=[SMEM, SMEM] + [VMEM] * count,
        out_specs=VMEM,
        scratch_shapes=[pltpu.VMEM((TILES, BR + 1, B, W), F32)],
        compiler_params=params(6),
        cost_estimate=cost(4 * ROWS * HALF * W * count, count * 3 * MIB),
        name="widen",
    )(table, places, *halves)


def product(halves, table, places, lists, right_side):
    count = len(halves)
    sizes = [array.shape[0] for array in lists] + [count]
    first = sum(sizes) - count

    def kernel(table_ref, places_ref, *refs):
        packed, refs = refs[:count], refs[count:]
        right_ref, *parts, dense_ref, sum_ref, rows, wide, sem = refs
        parts.append(wide)
        for k in range(count):
            unpack(packed[k], half_start(table_ref, first + k), places_ref, rows, wide.at[k])
        put = pltpu.make_async_copy(wide, dense_ref, sem)
        put.start()

        @pl.loop(0, ROWS // STEP)
        def _(i):
            part = pl.ds(pl.multiple_of(i * STEP, STEP), STEP)
            at, total = 0, None
            for ref, size in zip(parts, sizes):
                for k in range(size):
                    term = jnp.dot(ref[k, part, :], right_ref[at], preferred_element_type=F32)
                    at, total = at + 1, term if total is None else total + term
            sum_ref[part, :] = total

        put.wait()

    return pl.pallas_call(
        kernel,
        out_shape=(
            jax.ShapeDtypeStruct((count, ROWS, HALF), BF16),
            jax.ShapeDtypeStruct((ROWS, 2 * W), F32),
        ),
        in_specs=[SMEM, SMEM] + [VMEM] * (count + 1 + len(lists)),
        out_specs=(HBM, VMEM),
        scratch_shapes=[
            pltpu.VMEM((TILES, BR + 1, B, W), F32),
            pltpu.VMEM((count, ROWS, HALF), BF16),
            pltpu.SemaphoreType.DMA,
        ],
        compiler_params=params(12),
        cost_estimate=cost(16 * ROWS * HALF * W, 12 * MIB),
        name="product",
    )(table, places, *halves, right_side, *lists)


STEP = 256


def close_kernel(
    table_ref, places_ref, packed_ref, right_ref, sum_ref, dense_ref, mine_ref, other_ref, rows, wide, sem
):
    unpack(packed_ref, half_start(table_ref, FIRST), places_ref, rows, wide.at[0])
    put = pltpu.make_async_copy(wide, dense_ref, sem)
    put.start()
    total = jnp.dot(wide[0], right_ref[FIRST], preferred_element_type=F32) + sum_ref[...]
    mine_ref[...] = total[:, :W]
    other_ref[...] = total[:, W:]
    put.wait()


def close(packed, table, places, right_side, total):
    return pl.pallas_call(
        close_kernel,
        out_shape=(jax.ShapeDtypeStruct((1, ROWS, HALF), BF16),)
        + (jax.ShapeDtypeStruct((ROWS, W), F32),) * 2,
        in_specs=[SMEM, SMEM, VMEM, VMEM, VMEM],
        out_specs=(HBM, VMEM, VMEM),
        scratch_shapes=[
            pltpu.VMEM((TILES, BR + 1, B, W), F32),
            pltpu.VMEM((1, ROWS, HALF), BF16),
            pltpu.SemaphoreType.DMA,
        ],
        compiler_params=params(12),
        cost_estimate=cost(4 * ROWS * HALF * W, 3 * MIB),
        name="close",
    )(table, places, packed, right_side, total)


def finish_kernel(mine_ref, other_ref, masks_ref, square_ref):
    scale = (NB / (KX * KX * B)) ** 0.5
    for i in range(BR):
        rows = pl.ds(i * B, B)
        keep = jnp.broadcast_to(masks_ref[1, i : i + 1, :], (B, W))
        value = (mine_ref[rows, :] + other_ref[rows, :]) * scale
        square_ref[rows, :] = jnp.where(keep > 0.0, value, 0.0).astype(BF16)


def finish(mine, other, masks):
    return pl.pallas_call(
        finish_kernel,
        out_shape=jax.ShapeDtypeStruct((ROWS, W), BF16),
        in_specs=[VMEM] * 3,
        out_specs=VMEM,
        compiler_params=params(4),
        cost_estimate=cost(400_000, MIB),
        name="finish",
    )(mine, other, masks)


def cube_kernel(table_ref, *refs):
    *lists, square_hbm, tile_ref, masks_ref, out_ref, acc, square_ref, held, sems = refs
    scale = (NB / (KX * KSQ * B)) ** 0.5
    first = pltpu.make_async_copy(square_hbm, square_ref, sems.at[len(lists)])
    first.start()
    fetches, begins, start = [], [], 0
    for at, ref in enumerate(lists):
        count = ref.shape[0]
        fetches.append(pltpu.make_async_copy(ref, held.at[pl.ds(start, count)], sems.at[at]))
        fetches[-1].start()
        begins.append(start)
        start += count
    first.wait()
    for ref, fetch, begin in zip(lists, fetches, begins):
        fetch.wait()
        for k in range(begin, begin + ref.shape[0]):
            g, core = table_ref[2 * k], table_ref[2 * k + 1]
            half = square_ref[g, pl.ds(pl.multiple_of(core * HALF, HALF), HALF), :]
            term = jnp.dot(held[k], half, preferred_element_type=F32)
            acc[...] = term if k == 0 else acc[...] + term
    for k in range(BR):
        rows = pl.ds(k * B, B)
        keep_x = jnp.broadcast_to(masks_ref[0, k : k + 1, :], (B, W))
        keep_out = jnp.broadcast_to(masks_ref[2, k : k + 1, :], (B, W))
        sparse = jnp.where(keep_x > 0.0, tile_ref[rows, :].astype(F32), 0.0)
        result = 1.5 * sparse - 0.5 * (acc[rows, :] * scale)
        out_ref[rows, :] = jnp.where(keep_out > 0.0, result, 0.0).astype(BF16)


def cube(table, lists, squares, tile, masks):
    return pl.pallas_call(
        cube_kernel,
        out_shape=jax.ShapeDtypeStruct((ROWS, W), BF16),
        in_specs=[SMEM] + [HBM] * (len(lists) + 1) + [VMEM] * 2,
        out_specs=VMEM,
        scratch_shapes=[
            pltpu.VMEM((ROWS, W), F32),
            pltpu.VMEM((GROUPS, ROWS, W), BF16),
            pltpu.VMEM((2 * (FIRST + 1), ROWS, HALF), BF16),
            pltpu.SemaphoreType.DMA((len(lists) + 1,)),
        ],
        compiler_params=params(60),
        cost_estimate=cost(2 * GROUPS * ROWS * ROWS * W, 20 * MIB),
        name="cube",
    )(table, *lists, squares, tile, masks)


def local(matrix, list_x, list_sq, list_out):
    layers = lax.axis_size("layer")
    col = lax.axis_index("col").astype(jnp.int32)
    layer = lax.axis_index("layer").astype(jnp.int32)
    y, core = col // 2, col % 2
    sign = 1 - 2 * core
    base = jnp.reshape((col * layers + layer) * (W // B), (1,))

    brought = [(0, 1), (1, 1), (1, 0), (2, 1), (2, 0), (3, 1), (3, 0), (4, 1)]
    table = []
    for turn, own in ((-sign, core), (sign, 1 - core)):
        for d, same in brought:
            table += [jnp.bitwise_and(y + turn * d, GROUPS - 1), own if same else 1 - own]
    table = jnp.stack(table)

    cols = 2 * GROUPS
    swap = [(c, c ^ 1) for c in range(cols)]
    turn_y = [(c, (c + (2 if c % 2 == 0 else -2)) % cols) for c in range(cols)]

    def along_y(piece):
        return lax.ppermute(piece, "col", turn_y)

    def across(piece):
        return lax.ppermute(piece, "col", swap)

    def after(piece, *done):
        return lax.optimization_barrier((piece, *done))[0]

    pay, left, places = pack(base, list_x, matrix)
    pays = lax.all_gather(pay, "row", axis=0, tiled=False)
    a0 = lax.all_to_all(left, "layer", 0, 0, tiled=True)
    b0 = across(a0)
    a1, b1 = along_y(a0), along_y(b0)
    masks = masks_of(base, (list_x, list_sq, list_out))
    lists = [widen(0, [after(a0, masks)], table, places)]
    a2, b2 = along_y(after(a1, lists[-1])), along_y(b1)
    lists.append(widen(1, [a1, b1], table, places))
    a3, b3 = along_y(after(a2, lists[-1])), along_y(b2)
    lists.append(widen(3, [a2, b2], table, places))
    a4 = along_y(after(a3, lists[-1]))
    pays = after(pays, lists[-1], a3, b3)
    right_side = right(table, pays, across(pays))
    dense, total = product([a3, b3], table, places, lists, right_side)
    end, mine, other = close(a4, table, places, right_side, total)
    square = finish(mine, across(other), masks)

    squares = lax.all_gather(square, "row", axis=0, tiled=False)
    lists += [dense, end]
    lists += [across(part) for part in lists]
    return cube(table, lists, squares, matrix, masks)


def solution(mesh):
    placed = (P("row", ("col", "layer")), P("row", None), P("row", None), P("row", None))
    return jax.shard_map(
        local, mesh=mesh, in_specs=placed, out_specs=P("row", ("col", "layer")), check_vma=False
    )
```

```python
import jax
import jax.numpy as jnp
from jax import lax
from jax.experimental import pallas as pl
from jax.experimental.pallas import tpu as pltpu
from jax.sharding import PartitionSpec as P

B = 32
NB = 256
KX = 40
KSQ = 60
CAP = 10
ROWS = 1024
W = 128
BR = ROWS // B
GROUPS = 8
TILES = 4
HALF = TILES * W
PAY = 576
FIRST = 2 * TILES - 1
F32 = jnp.float32
BF16 = jnp.bfloat16
MIB = 1 << 20
SMEM = pl.BlockSpec(memory_space=pltpu.SMEM)
VMEM = pl.BlockSpec(memory_space=pltpu.VMEM)
HBM = pl.BlockSpec(memory_space=pltpu.HBM)


def params(limit):
    return pltpu.CompilerParams(vmem_limit_bytes=limit * MIB)


def cost(flops, size):
    return pl.CostEstimate(flops=flops, bytes_accessed=size, transcendentals=0)


def copies_in(pairs, sems):
    copies = [pltpu.make_async_copy(a, b, sems.at[k]) for k, (a, b) in enumerate(pairs)]
    for copy in copies:
        copy.start()
    for copy in copies:
        copy.wait()


def lane_hits(lists, base):
    ids = base + lax.broadcasted_iota(jnp.int32, (BR, W), 1) // B
    hit = jnp.zeros((BR, W), F32)
    for t in range(lists.shape[1]):
        hit = jnp.where(lists[:, t : t + 1] == ids, 1.0, hit)
    return hit


def slots_of(hit):
    below = lax.broadcasted_iota(jnp.int32, (BR, BR), 1) < lax.broadcasted_iota(
        jnp.int32, (BR, BR), 0
    )
    rank = jnp.dot(
        jnp.where(below, 1.0, 0.0).astype(BF16), hit.astype(BF16), preferred_element_type=F32
    )
    return jnp.where(hit > 0.0, rank, float(CAP))


def pack_kernel(base_ref, list_hbm, tile_hbm, pay_ref, left_ref, places_ref, list_ref, tile_ref, sems):
    copies_in([(list_hbm, list_ref), (tile_hbm, tile_ref)], sems)
    lists = list_ref[...]
    hit = lane_hits(lists, base_ref[0])
    slot = slots_of(hit)
    slot_int = slot.astype(jnp.int32)
    packed = [jnp.zeros((B, W), F32) for _ in range(CAP)]
    for i in range(BR):
        block = tile_ref[pl.ds(i * B, B), :].astype(F32)
        row = jnp.broadcast_to(slot_int[i : i + 1, :], (B, W))
        for s in range(min(i + 1, CAP)):
            packed[s] = jnp.where(row == s, block, packed[s])
    for s in range(CAP):
        value = packed[s].astype(BF16)
        pay_ref[pl.ds(s * B, B), :] = value
        for x in range(TILES):
            left_ref[x, s] = value
    pay_ref[pl.ds(CAP * B, B), :] = slot.astype(BF16)
    pay_ref[pl.ds((CAP + 1) * B, PAY - (CAP + 1) * B), :] = jnp.zeros(
        (PAY - (CAP + 1) * B, W), BF16
    )

    ids = lax.broadcasted_iota(jnp.int32, (BR, NB), 1)
    every = jnp.zeros((BR, NB), F32)
    for t in range(KX):
        every = jnp.where(lists[:, t : t + 1] == ids, 1.0, every)
    slot = slots_of(every)
    rows = lax.broadcasted_iota(jnp.int32, (BR, NB), 0).astype(F32) - BR
    for s in range(CAP):
        at = jnp.sum(jnp.where(slot == s, rows, 0.0), axis=0, keepdims=True) + BR
        places_ref[pl.ds(s, 1), :] = at.astype(jnp.int32)


def pack(base, list_x, tile):
    return pl.pallas_call(
        pack_kernel,
        out_shape=(
            jax.ShapeDtypeStruct((PAY, W), BF16),
            jax.ShapeDtypeStruct((TILES, CAP, B, W), BF16),
            jax.ShapeDtypeStruct((CAP, NB), jnp.int32),
        ),
        in_specs=[SMEM, HBM, HBM],
        out_specs=(VMEM,) * 3,
        scratch_shapes=[
            pltpu.VMEM((BR, KX), jnp.int32),
            pltpu.VMEM((ROWS, W), BF16),
            pltpu.SemaphoreType.DMA((2,)),
        ],
        compiler_params=params(6),
        cost_estimate=cost(10_000_000, 500_000),
        name="pack",
    )(base, list_x, tile)


def masks_kernel(base_ref, x_ref, sq_ref, out_ref, masks_ref):
    for k, lists in enumerate((x_ref, sq_ref, out_ref)):
        masks_ref[k] = lane_hits(lists[...], base_ref[0])


def masks_of(base, lists):
    return pl.pallas_call(
        masks_kernel,
        out_shape=jax.ShapeDtypeStruct((3, BR, W), F32),
        in_specs=[SMEM] + [VMEM] * 3,
        out_specs=VMEM,
        compiler_params=params(4),
        cost_estimate=cost(1_000_000, 100_000),
        name="masks",
    )(base, *lists)


def right_kernel(table_ref, mine_hbm, other_hbm, right_ref, pays_ref, sems):
    rows = pl.ds(0, (CAP + 1) * B)
    pairs = [(ref.at[:, rows], pays_ref.at[k]) for k, ref in enumerate((mine_hbm, other_hbm))]
    copies_in(pairs, sems)

    @pl.loop(0, 2 * TILES)
    def _(h):
        g, core = table_ref[2 * h], table_ref[2 * h + 1]
        first = pl.multiple_of(CAP * B + core * (BR // 2), BR // 2)
        for k in range(2):
            part = [pays_ref[k, g, pl.ds(s * B, B), :].astype(F32) for s in range(CAP)]
            slot = pays_ref[k, g, pl.ds(first, BR // 2), :].astype(F32).astype(jnp.int32)
            for t in range(BR // 2):
                row = jnp.broadcast_to(slot[t : t + 1, :], (B, W))
                value = jnp.zeros((B, W), F32)
                for s in range(CAP):
                    value = jnp.where(row == s, part[s], value)
                right_ref[h, pl.ds(t * B, B), pl.ds(k * W, W)] = value.astype(BF16)


def right(table, mine, other):
    return pl.pallas_call(
        right_kernel,
        out_shape=jax.ShapeDtypeStruct((2 * TILES, HALF, 2 * W), BF16),
        in_specs=[SMEM] + [HBM] * 2,
        out_specs=VMEM,
        scratch_shapes=[
            pltpu.VMEM((2, GROUPS, (CAP + 1) * B, W), BF16),
            pltpu.SemaphoreType.DMA((2,)),
        ],
        compiler_params=params(12),
        cost_estimate=cost(40_000_000, 4 * MIB),
        name="right",
    )(table, mine, other)


def unpack(packed_ref, start, places_ref, rows, wide):
    lane = lax.broadcasted_iota(jnp.int32, (B, W), 1) // B
    masks = [lane == c for c in range(W // B)]
    for q in range(TILES):
        rows[q, pl.ds(0, BR)] = jnp.zeros((BR, B, W), F32)
    for q in range(TILES):
        for s in range(CAP):
            block = packed_ref[q, s].astype(F32)
            for c in range(W // B):
                row = places_ref[s, start + q * (W // B) + c]
                pltpu.store(rows.at[q, row], block, mask=masks[c])
    for q in range(TILES):
        for i in range(BR):
            wide[pl.ds(i * B, B), pl.ds(q * W, W)] = rows[q, i].astype(BF16)


def half_start(table_ref, k):
    return (table_ref[2 * k] * 2 + table_ref[2 * k + 1]) * (HALF // B)


def widen(first, halves, table, places):
    count = len(halves)

    def kernel(table_ref, places_ref, *refs):
        dense_ref, rows = refs[count:]
        for k in range(count):
            unpack(refs[k], half_start(table_ref, first + k), places_ref, rows, dense_ref.at[k])

    return pl.pallas_call(
        kernel,
        out_shape=jax.ShapeDtypeStruct((count, ROWS, HALF), BF16),
        in_specs=[SMEM, SMEM] + [VMEM] * count,
        out_specs=VMEM,
        scratch_shapes=[pltpu.VMEM((TILES, BR + 1, B, W), F32)],
        compiler_params=params(6),
        cost_estimate=cost(4 * ROWS * HALF * W * count, count * 3 * MIB),
        name="widen",
    )(table, places, *halves)


def product(halves, table, places, lists, right_side):
    count = len(halves)
    sizes = [array.shape[0] for array in lists] + [count]
    first = sum(sizes) - count

    def kernel(table_ref, places_ref, *refs):
        packed, refs = refs[:count], refs[count:]
        right_ref, *parts, dense_ref, sum_ref, rows, wide, sem = refs
        parts.append(wide)
        for k in range(count):
            unpack(packed[k], half_start(table_ref, first + k), places_ref, rows, wide.at[k])
        put = pltpu.make_async_copy(wide, dense_ref, sem)
        put.start()

        @pl.loop(0, ROWS // STEP)
        def _(i):
            part = pl.ds(pl.multiple_of(i * STEP, STEP), STEP)
            at, total = 0, None
            for ref, size in zip(parts, sizes):
                for k in range(size):
                    term = jnp.dot(ref[k, part, :], right_ref[at], preferred_element_type=F32)
                    at, total = at + 1, term if total is None else total + term
            sum_ref[part, :] = total

        put.wait()

    return pl.pallas_call(
        kernel,
        out_shape=(
            jax.ShapeDtypeStruct((count, ROWS, HALF), BF16),
            jax.ShapeDtypeStruct((ROWS, 2 * W), F32),
        ),
        in_specs=[SMEM, SMEM] + [VMEM] * (count + 1 + len(lists)),
        out_specs=(HBM, VMEM),
        scratch_shapes=[
            pltpu.VMEM((TILES, BR + 1, B, W), F32),
            pltpu.VMEM((count, ROWS, HALF), BF16),
            pltpu.SemaphoreType.DMA,
        ],
        compiler_params=params(12),
        cost_estimate=cost(16 * ROWS * HALF * W, 12 * MIB),
        name="product",
    )(table, places, *halves, right_side, *lists)


STEP = 256


def close_kernel(
    table_ref, places_ref, packed_ref, right_ref, sum_ref, dense_ref, mine_ref, other_ref, rows, wide, sem
):
    unpack(packed_ref, half_start(table_ref, FIRST), places_ref, rows, wide.at[0])
    put = pltpu.make_async_copy(wide, dense_ref, sem)
    put.start()
    total = jnp.dot(wide[0], right_ref[FIRST], preferred_element_type=F32) + sum_ref[...]
    mine_ref[...] = total[:, :W]
    other_ref[...] = total[:, W:]
    put.wait()


def close(packed, table, places, right_side, total):
    return pl.pallas_call(
        close_kernel,
        out_shape=(jax.ShapeDtypeStruct((1, ROWS, HALF), BF16),)
        + (jax.ShapeDtypeStruct((ROWS, W), F32),) * 2,
        in_specs=[SMEM, SMEM, VMEM, VMEM, VMEM],
        out_specs=(HBM, VMEM, VMEM),
        scratch_shapes=[
            pltpu.VMEM((TILES, BR + 1, B, W), F32),
            pltpu.VMEM((1, ROWS, HALF), BF16),
            pltpu.SemaphoreType.DMA,
        ],
        compiler_params=params(12),
        cost_estimate=cost(4 * ROWS * HALF * W, 3 * MIB),
        name="close",
    )(table, places, packed, right_side, total)


def finish_kernel(mine_ref, other_ref, masks_ref, square_ref):
    scale = (NB / (KX * KX * B)) ** 0.5
    for i in range(BR):
        rows = pl.ds(i * B, B)
        keep = jnp.broadcast_to(masks_ref[1, i : i + 1, :], (B, W))
        value = (mine_ref[rows, :] + other_ref[rows, :]) * scale
        square_ref[rows, :] = jnp.where(keep > 0.0, value, 0.0).astype(BF16)


def finish(mine, other, masks):
    return pl.pallas_call(
        finish_kernel,
        out_shape=jax.ShapeDtypeStruct((ROWS, W), BF16),
        in_specs=[VMEM] * 3,
        out_specs=VMEM,
        compiler_params=params(4),
        cost_estimate=cost(400_000, MIB),
        name="finish",
    )(mine, other, masks)


AHEAD = 2


def cube_kernel(table_ref, *refs):
    *lists, square_hbm, tile_ref, masks_ref, out_ref, acc, square_ref, held, sems = refs
    scale = (NB / (KX * KSQ * B)) ** 0.5
    first = pltpu.make_async_copy(square_hbm, square_ref, sems.at[len(lists)])
    first.start()
    fetches, begins, start = [], [], 0
    for at, ref in enumerate(lists):
        count = ref.shape[0]
        fetches.append(pltpu.make_async_copy(ref, held.at[pl.ds(start, count)], sems.at[at]))
        begins.append(start)
        start += count
    for fetch in fetches[:AHEAD]:
        fetch.start()
    first.wait()
    for at, (ref, fetch, begin) in enumerate(zip(lists, fetches, begins)):
        fetch.wait()
        if at + AHEAD < len(fetches):
            fetches[at + AHEAD].start()
        for k in range(begin, begin + ref.shape[0]):
            g, core = table_ref[2 * k], table_ref[2 * k + 1]
            half = square_ref[g, pl.ds(pl.multiple_of(core * HALF, HALF), HALF), :]
            term = jnp.dot(held[k], half, preferred_element_type=F32)
            acc[...] = term if k == 0 else acc[...] + term
    for k in range(BR):
        rows = pl.ds(k * B, B)
        keep_x = jnp.broadcast_to(masks_ref[0, k : k + 1, :], (B, W))
        keep_out = jnp.broadcast_to(masks_ref[2, k : k + 1, :], (B, W))
        sparse = jnp.where(keep_x > 0.0, tile_ref[rows, :].astype(F32), 0.0)
        result = 1.5 * sparse - 0.5 * (acc[rows, :] * scale)
        out_ref[rows, :] = jnp.where(keep_out > 0.0, result, 0.0).astype(BF16)


def cube(table, lists, squares, tile, masks):
    return pl.pallas_call(
        cube_kernel,
        out_shape=jax.ShapeDtypeStruct((ROWS, W), BF16),
        in_specs=[SMEM] + [HBM] * (len(lists) + 1) + [VMEM] * 2,
        out_specs=VMEM,
        scratch_shapes=[
            pltpu.VMEM((ROWS, W), F32),
            pltpu.VMEM((GROUPS, ROWS, W), BF16),
            pltpu.VMEM((2 * (FIRST + 1), ROWS, HALF), BF16),
            pltpu.SemaphoreType.DMA((len(lists) + 1,)),
        ],
        compiler_params=params(60),
        cost_estimate=cost(2 * GROUPS * ROWS * ROWS * W, 20 * MIB),
        name="cube",
    )(table, *lists, squares, tile, masks)


def local(matrix, list_x, list_sq, list_out):
    layers = lax.axis_size("layer")
    col = lax.axis_index("col").astype(jnp.int32)
    layer = lax.axis_index("layer").astype(jnp.int32)
    y, core = col // 2, col % 2
    sign = 1 - 2 * core
    base = jnp.reshape((col * layers + layer) * (W // B), (1,))

    brought = [(0, 1), (1, 1), (1, 0), (2, 1), (2, 0), (3, 1), (3, 0), (4, 1)]
    table = []
    for turn, own in ((-sign, core), (sign, 1 - core)):
        for d, same in brought:
            table += [jnp.bitwise_and(y + turn * d, GROUPS - 1), own if same else 1 - own]
    table = jnp.stack(table)

    cols = 2 * GROUPS
    swap = [(c, c ^ 1) for c in range(cols)]
    turn_y = [(c, (c + (2 if c % 2 == 0 else -2)) % cols) for c in range(cols)]

    def along_y(piece):
        return lax.ppermute(piece, "col", turn_y)

    def across(piece):
        return lax.ppermute(piece, "col", swap)

    def after(piece, *done):
        return lax.optimization_barrier((piece, *done))[0]

    pay, left, places = pack(base, list_x, matrix)
    pays = lax.all_gather(pay, "row", axis=0, tiled=False)
    a0 = lax.all_to_all(left, "layer", 0, 0, tiled=True)
    b0 = across(a0)
    a1, b1 = along_y(a0), along_y(b0)
    masks = masks_of(base, (list_x, list_sq, list_out))
    lists = [widen(0, [after(a0, masks)], table, places)]
    a2, b2 = along_y(after(a1, lists[-1])), along_y(b1)
    lists.append(widen(1, [a1, b1], table, places))
    a3, b3 = along_y(after(a2, lists[-1])), along_y(b2)
    lists.append(widen(3, [a2, b2], table, places))
    a4 = along_y(after(a3, lists[-1]))
    pays = after(pays, lists[-1], a3, b3)
    right_side = right(table, pays, across(pays))
    dense, total = product([a3, b3], table, places, lists, right_side)
    end, mine, other = close(a4, table, places, right_side, total)
    square = finish(mine, across(other), masks)

    squares = lax.all_gather(square, "row", axis=0, tiled=False)
    lists += [dense, end]
    lists += [across(part) for part in lists]
    return cube(table, lists, squares, matrix, masks)


def solution(mesh):
    placed = (P("row", ("col", "layer")), P("row", None), P("row", None), P("row", None))
    return jax.shard_map(
        local, mesh=mesh, in_specs=placed, out_specs=P("row", ("col", "layer")), check_vma=False
    )
```

```python
import jax
import jax.numpy as jnp
from jax import lax
from jax.experimental import pallas as pl
from jax.experimental.pallas import tpu as pltpu
from jax.sharding import PartitionSpec as P

B = 32
NB = 256
KX = 40
KSQ = 60
CAP = 10
ROWS = 1024
W = 128
BR = ROWS // B
GROUPS = 8
TILES = 4
HALF = TILES * W
PAY = 576
FIRST = 2 * TILES - 1
F32 = jnp.float32
BF16 = jnp.bfloat16
MIB = 1 << 20
SMEM = pl.BlockSpec(memory_space=pltpu.SMEM)
VMEM = pl.BlockSpec(memory_space=pltpu.VMEM)
HBM = pl.BlockSpec(memory_space=pltpu.HBM)


def params(limit):
    return pltpu.CompilerParams(vmem_limit_bytes=limit * MIB)


def cost(flops, size):
    return pl.CostEstimate(flops=flops, bytes_accessed=size, transcendentals=0)


def copies_in(pairs, sems):
    copies = [pltpu.make_async_copy(a, b, sems.at[k]) for k, (a, b) in enumerate(pairs)]
    for copy in copies:
        copy.start()
    for copy in copies:
        copy.wait()


def lane_hits(lists, base):
    ids = base + lax.broadcasted_iota(jnp.int32, (BR, W), 1) // B
    hit = jnp.zeros((BR, W), F32)
    for t in range(lists.shape[1]):
        hit = jnp.where(lists[:, t : t + 1] == ids, 1.0, hit)
    return hit


def slots_of(hit):
    below = lax.broadcasted_iota(jnp.int32, (BR, BR), 1) < lax.broadcasted_iota(
        jnp.int32, (BR, BR), 0
    )
    rank = jnp.dot(
        jnp.where(below, 1.0, 0.0).astype(BF16), hit.astype(BF16), preferred_element_type=F32
    )
    return jnp.where(hit > 0.0, rank, float(CAP))


def pack_kernel(base_ref, list_hbm, tile_hbm, pay_ref, left_ref, places_ref, list_ref, tile_ref, sems):
    copies_in([(list_hbm, list_ref), (tile_hbm, tile_ref)], sems)
    lists = list_ref[...]
    hit = lane_hits(lists, base_ref[0])
    slot = slots_of(hit)
    slot_int = slot.astype(jnp.int32)
    packed = [jnp.zeros((B, W), F32) for _ in range(CAP)]
    for i in range(BR):
        block = tile_ref[pl.ds(i * B, B), :].astype(F32)
        row = jnp.broadcast_to(slot_int[i : i + 1, :], (B, W))
        for s in range(min(i + 1, CAP)):
            packed[s] = jnp.where(row == s, block, packed[s])
    for s in range(CAP):
        value = packed[s].astype(BF16)
        pay_ref[pl.ds(s * B, B), :] = value
        for x in range(TILES):
            left_ref[x, s] = value
    pay_ref[pl.ds(CAP * B, B), :] = slot.astype(BF16)
    pay_ref[pl.ds((CAP + 1) * B, PAY - (CAP + 1) * B), :] = jnp.zeros(
        (PAY - (CAP + 1) * B, W), BF16
    )

    ids = lax.broadcasted_iota(jnp.int32, (BR, NB), 1)
    every = jnp.zeros((BR, NB), F32)
    for t in range(KX):
        every = jnp.where(lists[:, t : t + 1] == ids, 1.0, every)
    slot = slots_of(every)
    rows = lax.broadcasted_iota(jnp.int32, (BR, NB), 0).astype(F32) - BR
    for s in range(CAP):
        at = jnp.sum(jnp.where(slot == s, rows, 0.0), axis=0, keepdims=True) + BR
        places_ref[pl.ds(s, 1), :] = at.astype(jnp.int32)


def pack(base, list_x, tile):
    return pl.pallas_call(
        pack_kernel,
        out_shape=(
            jax.ShapeDtypeStruct((PAY, W), BF16),
            jax.ShapeDtypeStruct((TILES, CAP, B, W), BF16),
            jax.ShapeDtypeStruct((CAP, NB), jnp.int32),
        ),
        in_specs=[SMEM, HBM, HBM],
        out_specs=(VMEM,) * 3,
        scratch_shapes=[
            pltpu.VMEM((BR, KX), jnp.int32),
            pltpu.VMEM((ROWS, W), BF16),
            pltpu.SemaphoreType.DMA((2,)),
        ],
        compiler_params=params(6),
        cost_estimate=cost(10_000_000, 500_000),
        name="pack",
    )(base, list_x, tile)


def masks_kernel(base_ref, x_ref, sq_ref, out_ref, masks_ref):
    for k, lists in enumerate((x_ref, sq_ref, out_ref)):
        masks_ref[k] = lane_hits(lists[...], base_ref[0])


def masks_of(base, lists):
    return pl.pallas_call(
        masks_kernel,
        out_shape=jax.ShapeDtypeStruct((3, BR, W), F32),
        in_specs=[SMEM] + [VMEM] * 3,
        out_specs=VMEM,
        compiler_params=params(4),
        cost_estimate=cost(1_000_000, 100_000),
        name="masks",
    )(base, *lists)


def right_kernel(table_ref, mine_hbm, other_hbm, right_ref, pays_ref, sems):
    rows = pl.ds(0, (CAP + 1) * B)
    pairs = [(ref.at[:, rows], pays_ref.at[k]) for k, ref in enumerate((mine_hbm, other_hbm))]
    copies_in(pairs, sems)

    @pl.loop(0, 2 * TILES)
    def _(h):
        g, core = table_ref[2 * h], table_ref[2 * h + 1]
        first = pl.multiple_of(CAP * B + core * (BR // 2), BR // 2)
        for k in range(2):
            part = [pays_ref[k, g, pl.ds(s * B, B), :].astype(F32) for s in range(CAP)]
            slot = pays_ref[k, g, pl.ds(first, BR // 2), :].astype(F32).astype(jnp.int32)
            for t in range(BR // 2):
                row = jnp.broadcast_to(slot[t : t + 1, :], (B, W))
                value = jnp.zeros((B, W), F32)
                for s in range(CAP):
                    value = jnp.where(row == s, part[s], value)
                right_ref[h, pl.ds(t * B, B), pl.ds(k * W, W)] = value.astype(BF16)


def right(table, mine, other):
    return pl.pallas_call(
        right_kernel,
        out_shape=jax.ShapeDtypeStruct((2 * TILES, HALF, 2 * W), BF16),
        in_specs=[SMEM] + [HBM] * 2,
        out_specs=VMEM,
        scratch_shapes=[
            pltpu.VMEM((2, GROUPS, (CAP + 1) * B, W), BF16),
            pltpu.SemaphoreType.DMA((2,)),
        ],
        compiler_params=params(12),
        cost_estimate=cost(40_000_000, 4 * MIB),
        name="right",
    )(table, mine, other)


def unpack(packed_ref, start, places_ref, rows, wide):
    lane = lax.broadcasted_iota(jnp.int32, (B, W), 1) // B
    masks = [lane == c for c in range(W // B)]
    for q in range(TILES):
        rows[q, pl.ds(0, BR)] = jnp.zeros((BR, B, W), F32)
    for q in range(TILES):
        for s in range(CAP):
            block = packed_ref[q, s].astype(F32)
            for c in range(W // B):
                row = places_ref[s, start + q * (W // B) + c]
                pltpu.store(rows.at[q, row], block, mask=masks[c])
    for q in range(TILES):
        for i in range(BR):
            wide[pl.ds(i * B, B), pl.ds(q * W, W)] = rows[q, i].astype(BF16)


def half_start(table_ref, k):
    return (table_ref[2 * k] * 2 + table_ref[2 * k + 1]) * (HALF // B)


def widen(first, halves, table, places):
    count = len(halves)

    def kernel(table_ref, places_ref, *refs):
        dense_ref, rows = refs[count:]
        for k in range(count):
            unpack(refs[k], half_start(table_ref, first + k), places_ref, rows, dense_ref.at[k])

    return pl.pallas_call(
        kernel,
        out_shape=jax.ShapeDtypeStruct((count, ROWS, HALF), BF16),
        in_specs=[SMEM, SMEM] + [VMEM] * count,
        out_specs=VMEM,
        scratch_shapes=[pltpu.VMEM((TILES, BR + 1, B, W), F32)],
        compiler_params=params(6),
        cost_estimate=cost(4 * ROWS * HALF * W * count, count * 3 * MIB),
        name="widen",
    )(table, places, *halves)


def product(halves, table, places, lists, right_side):
    count = len(halves)
    sizes = [array.shape[0] for array in lists] + [count]
    first = sum(sizes) - count

    def kernel(table_ref, places_ref, *refs):
        packed, refs = refs[:count], refs[count:]
        right_ref, *parts, dense_ref, sum_ref, rows, wide, sem = refs
        parts.append(wide)
        for k in range(count):
            unpack(packed[k], half_start(table_ref, first + k), places_ref, rows, wide.at[k])
        put = pltpu.make_async_copy(wide, dense_ref, sem)
        put.start()

        @pl.loop(0, ROWS // STEP)
        def _(i):
            part = pl.ds(pl.multiple_of(i * STEP, STEP), STEP)
            at, total = 0, None
            for ref, size in zip(parts, sizes):
                for k in range(size):
                    term = jnp.dot(ref[k, part, :], right_ref[at], preferred_element_type=F32)
                    at, total = at + 1, term if total is None else total + term
            sum_ref[part, :] = total

        put.wait()

    return pl.pallas_call(
        kernel,
        out_shape=(
            jax.ShapeDtypeStruct((count, ROWS, HALF), BF16),
            jax.ShapeDtypeStruct((ROWS, 2 * W), F32),
        ),
        in_specs=[SMEM, SMEM] + [VMEM] * (count + 1 + len(lists)),
        out_specs=(HBM, VMEM),
        scratch_shapes=[
            pltpu.VMEM((TILES, BR + 1, B, W), F32),
            pltpu.VMEM((count, ROWS, HALF), BF16),
            pltpu.SemaphoreType.DMA,
        ],
        compiler_params=params(12),
        cost_estimate=cost(16 * ROWS * HALF * W, 12 * MIB),
        name="product",
    )(table, places, *halves, right_side, *lists)


STEP = 256


def close_kernel(
    table_ref, places_ref, packed_ref, right_ref, sum_ref, dense_ref, mine_ref, other_ref, rows, wide, sem
):
    unpack(packed_ref, half_start(table_ref, FIRST), places_ref, rows, wide.at[0])
    put = pltpu.make_async_copy(wide, dense_ref, sem)
    put.start()
    total = jnp.dot(wide[0], right_ref[FIRST], preferred_element_type=F32) + sum_ref[...]
    mine_ref[...] = total[:, :W]
    other_ref[...] = total[:, W:]
    put.wait()


def close(packed, table, places, right_side, total):
    return pl.pallas_call(
        close_kernel,
        out_shape=(jax.ShapeDtypeStruct((1, ROWS, HALF), BF16),)
        + (jax.ShapeDtypeStruct((ROWS, W), F32),) * 2,
        in_specs=[SMEM, SMEM, VMEM, VMEM, VMEM],
        out_specs=(HBM, VMEM, VMEM),
        scratch_shapes=[
            pltpu.VMEM((TILES, BR + 1, B, W), F32),
            pltpu.VMEM((1, ROWS, HALF), BF16),
            pltpu.SemaphoreType.DMA,
        ],
        compiler_params=params(12),
        cost_estimate=cost(4 * ROWS * HALF * W, 3 * MIB),
        name="close",
    )(table, places, packed, right_side, total)


def finish_kernel(mine_ref, other_ref, masks_ref, square_ref):
    scale = (NB / (KX * KX * B)) ** 0.5
    for i in range(BR):
        rows = pl.ds(i * B, B)
        keep = jnp.broadcast_to(masks_ref[1, i : i + 1, :], (B, W))
        value = (mine_ref[rows, :] + other_ref[rows, :]) * scale
        square_ref[rows, :] = jnp.where(keep > 0.0, value, 0.0).astype(BF16)


def finish(mine, other, masks):
    return pl.pallas_call(
        finish_kernel,
        out_shape=jax.ShapeDtypeStruct((ROWS, W), BF16),
        in_specs=[VMEM] * 3,
        out_specs=VMEM,
        compiler_params=params(4),
        cost_estimate=cost(400_000, MIB),
        name="finish",
    )(mine, other, masks)


KEPT = 2


def cube_kernel(table_ref, *refs):
    *lists, square_hbm, tile_ref, masks_ref, out_ref, acc, square_ref, held, sems = refs
    scale = (NB / (KX * KSQ * B)) ** 0.5
    first = pltpu.make_async_copy(square_hbm, square_ref, sems.at[len(lists)])
    first.start()
    fetches, begins, start = [], [], 0
    for at, ref in enumerate(lists):
        count = ref.shape[0]
        fetch = pltpu.make_async_copy(ref, held.at[pl.ds(start, count)], sems.at[at])
        if at >= KEPT:
            fetch.start()
        fetches.append(fetch)
        begins.append(start)
        start += count
    first.wait()
    for at, (ref, fetch, begin) in enumerate(zip(lists, fetches, begins)):
        if at >= KEPT:
            fetch.wait()
        for k in range(begin, begin + ref.shape[0]):
            g, core = table_ref[2 * k], table_ref[2 * k + 1]
            half = square_ref[g, pl.ds(pl.multiple_of(core * HALF, HALF), HALF), :]
            left = held[k] if at >= KEPT else ref[k - begin]
            term = jnp.dot(left, half, preferred_element_type=F32)
            acc[...] = term if k == 0 else acc[...] + term
    for k in range(BR):
        rows = pl.ds(k * B, B)
        keep_x = jnp.broadcast_to(masks_ref[0, k : k + 1, :], (B, W))
        keep_out = jnp.broadcast_to(masks_ref[2, k : k + 1, :], (B, W))
        sparse = jnp.where(keep_x > 0.0, tile_ref[rows, :].astype(F32), 0.0)
        result = 1.5 * sparse - 0.5 * (acc[rows, :] * scale)
        out_ref[rows, :] = jnp.where(keep_out > 0.0, result, 0.0).astype(BF16)


def cube(table, lists, squares, tile, masks):
    return pl.pallas_call(
        cube_kernel,
        out_shape=jax.ShapeDtypeStruct((ROWS, W), BF16),
        in_specs=[SMEM] + [VMEM] * KEPT + [HBM] * (len(lists) + 1 - KEPT) + [VMEM] * 2,
        out_specs=VMEM,
        scratch_shapes=[
            pltpu.VMEM((ROWS, W), F32),
            pltpu.VMEM((GROUPS, ROWS, W), BF16),
            pltpu.VMEM((2 * (FIRST + 1), ROWS, HALF), BF16),
            pltpu.SemaphoreType.DMA((len(lists) + 1,)),
        ],
        compiler_params=params(52),
        cost_estimate=cost(2 * GROUPS * ROWS * ROWS * W, 20 * MIB),
        name="cube",
    )(table, *lists, squares, tile, masks)


def local(matrix, list_x, list_sq, list_out):
    layers = lax.axis_size("layer")
    col = lax.axis_index("col").astype(jnp.int32)
    layer = lax.axis_index("layer").astype(jnp.int32)
    y, core = col // 2, col % 2
    sign = 1 - 2 * core
    base = jnp.reshape((col * layers + layer) * (W // B), (1,))

    brought = [(0, 1), (1, 1), (1, 0), (2, 1), (2, 0), (3, 1), (3, 0), (4, 1)]
    table = []
    for turn, own in ((-sign, core), (sign, 1 - core)):
        for d, same in brought:
            table += [jnp.bitwise_and(y + turn * d, GROUPS - 1), own if same else 1 - own]
    table = jnp.stack(table)

    cols = 2 * GROUPS
    swap = [(c, c ^ 1) for c in range(cols)]
    turn_y = [(c, (c + (2 if c % 2 == 0 else -2)) % cols) for c in range(cols)]

    def along_y(piece):
        return lax.ppermute(piece, "col", turn_y)

    def across(piece):
        return lax.ppermute(piece, "col", swap)

    def after(piece, *done):
        return lax.optimization_barrier((piece, *done))[0]

    pay, left, places = pack(base, list_x, matrix)
    pays = lax.all_gather(pay, "row", axis=0, tiled=False)
    a0 = lax.all_to_all(left, "layer", 0, 0, tiled=True)
    b0 = across(a0)
    a1, b1 = along_y(a0), along_y(b0)
    masks = masks_of(base, (list_x, list_sq, list_out))
    lists = [widen(0, [after(a0, masks)], table, places)]
    a2, b2 = along_y(after(a1, lists[-1])), along_y(b1)
    lists.append(widen(1, [a1, b1], table, places))
    a3, b3 = along_y(after(a2, lists[-1])), along_y(b2)
    lists.append(widen(3, [a2, b2], table, places))
    a4 = along_y(after(a3, lists[-1]))
    pays = after(pays, lists[-1], a3, b3)
    right_side = right(table, pays, across(pays))
    dense, total = product([a3, b3], table, places, lists, right_side)
    end, mine, other = close(a4, table, places, right_side, total)
    square = finish(mine, across(other), masks)

    squares = lax.all_gather(square, "row", axis=0, tiled=False)
    lists += [dense, end]
    lists += [across(part) for part in lists]
    return cube(table, lists, squares, matrix, masks)


def solution(mesh):
    placed = (P("row", ("col", "layer")), P("row", None), P("row", None), P("row", None))
    return jax.shard_map(
        local, mesh=mesh, in_specs=placed, out_specs=P("row", ("col", "layer")), check_vma=False
    )
```
